512 devices in a mesh: terms: 16 (over y, core), sectors: 32 (over z, x).
Axes of the slice: x: 4, y: 8, z: 8, core: 2. Of those that a mesh axis runs over, the one named last changes fastest.
Arguments:
- wavefunction: bfloat16 [4096, 4096], P('terms', 'sectors')
- left_env: bfloat16 [32, 32, 128, 128], P('terms', 'sectors')
- right_env: bfloat16 [32, 32, 128, 128], P('terms', 'sectors')
- sector_size: int32 [32], replicated, may hold values from 64 to 128, as said below
Outputs:
- sigma_first: bfloat16 [4096, 4096], P('terms', 'sectors')
- sigma_second: bfloat16 [4096, 4096], P('terms', 'sectors')
The draws below stay inside these ranges and needn't reach their ends.
Inputs may be any that keep to these rules, and one draw needn't show every extreme that they name: `sector_size`: each block has between 64 and 128 live states; some block has exactly 128.
All inputs are finite; a program needn't handle non-finite values.
Results may differ from the reference program's by a relative error of at most 0.0069.
Values may be sent and summed in bfloat16 or wider, within the bound.
A program may use at most 64 MiB of HBM per device.

```python
import jax
import jax.numpy as jnp
from jax import lax

BLK = 128
NB = 32
TERMS = 32
DIM = 4096


def draw_sector_size(key, part):
    key = jax.random.fold_in(key, 11)
    first, second = jax.random.split(key)
    sizes = jax.random.randint(first, (NB,), BLK // 2, BLK + 1)
    where_full = jax.random.randint(second, (), 0, NB)
    return sizes.at[where_full].set(BLK).astype(jnp.int32)


def draw_wavefunction(key, part):
    key = jax.random.fold_in(key, 23)
    first = jax.random.fold_in(key, 0)
    values = jax.random.normal(first, (DIM, DIM), jnp.float32)
    steps = jnp.arange(DIM, dtype=jnp.float32) / (DIM - 1)
    rising = jnp.exp(jnp.log(3.0) * steps)
    values = values * rising[:, None] * rising[None, :] * 0.4
    return values.astype(jnp.bfloat16)


def identity_blocks():
    states = jnp.arange(BLK, dtype=jnp.int32)
    return (states[:, None] == states[None, :]).astype(jnp.float32)


def draw_left_env(key, part):
    key = jax.random.fold_in(key, 37)
    noise = jax.random.normal(key, (TERMS, NB, BLK, BLK), jnp.float32) / jnp.sqrt(jnp.float32(BLK))
    steps = jnp.arange(NB, dtype=jnp.float32) / max(NB - 1, 1)
    diag_scale = 0.5 * jnp.exp(jnp.log(4.0) * steps)
    values = noise + diag_scale[None, :, None, None] * identity_blocks()[None, None]
    return values.astype(jnp.bfloat16)


def draw_right_env(key, part):
    key = jax.random.fold_in(key, 41)
    noise = jax.random.normal(key, (TERMS, NB, BLK, BLK), jnp.float32)
    noise = noise / jnp.sqrt(jnp.float32(BLK * TERMS))
    values = noise + identity_blocks()[None, None] / TERMS
    return values.astype(jnp.bfloat16)


def setup_inputs(seed: int = 0) -> dict:
    streams_of = jax.random.split(jax.random.key(seed), 5)
    wavefunction = draw_wavefunction(jax.random.fold_in(streams_of[4], 71), 0)
    left_env = draw_left_env(jax.random.fold_in(streams_of[4], 71), 0)
    right_env = draw_right_env(jax.random.fold_in(streams_of[4], 71), 0)
    sector_size = draw_sector_size(jax.random.fold_in(streams_of[4], 71), 0)
    return dict(wavefunction=wavefunction, left_env=left_env, right_env=right_env, sector_size=sector_size)


def live_states(sector_size):
    states = jnp.arange(BLK, dtype=jnp.int32)
    return (states[None, :] < sector_size[:, None]).reshape(-1)


def apply_ham(vector, left_env, right_env, live):
    both_live = live[:, None] & live[None, :]
    masked = jnp.where(both_live, vector, jnp.zeros_like(vector))
    blocks = masked.astype(jnp.float32).reshape(NB, BLK, DIM)

    def one_term(total, envs):
        left_term, right_term = envs
        image = jnp.einsum('rab,rbc->rac', left_term.astype(jnp.float32), blocks).astype(jnp.bfloat16)
        image = image.reshape(DIM, NB, BLK).astype(jnp.float32)
        total = total + jnp.einsum('inb,nob->ino', image, right_term.astype(jnp.float32))
        return total, None

    total, _ = lax.scan(one_term, jnp.zeros((DIM, NB, BLK), jnp.float32), (left_env, right_env))
    total = total.reshape(DIM, DIM)
    return jnp.where(both_live, total, jnp.zeros_like(total)).astype(jnp.bfloat16)


def reference(wavefunction, left_env, right_env, sector_size):
    live = live_states(sector_size)
    both_live = live[:, None] & live[None, :]
    start = jnp.where(both_live, wavefunction, jnp.zeros_like(wavefunction)).astype(jnp.float32)
    sigma_first = apply_ham(wavefunction, left_env, right_env, live)
    first_wide = sigma_first.astype(jnp.float32)
    theta = jnp.sum(start * first_wide) / jnp.sum(start * start)
    correction = (first_wide - theta * start).astype(jnp.bfloat16)
    sigma_second = apply_ham(correction, left_env, right_env, live)
    return sigma_first, sigma_second
```

```python
import functools

import jax
import jax.numpy as jnp
from jax import lax
from jax.experimental import pallas as pl
from jax.experimental.pallas import tpu as pltpu
from jax.sharding import PartitionSpec as P

MESH = pl.DeviceIdType.MESH
BLK = 128
X, Y, Z = 4, 8, 8
OFFS = (0, -1, 1, -2, 2, -3, 3, 4)


def wrap(value, n):
    return lax.rem(value + 2 * n, n)


def device(x, y, z, c):
    return {"terms": 2 * y + c, "sectors": 4 * z + x}


def kernel(
    size_ref, v_hbm, l_hbm, r_hbm, out1, out2,
    lb, rz, rb, vt, vc, im, s1, g, s1h, gh, part, core_in, x_in, y_in, z_in,
    local_sem, lring_s, lring_r, lx_s, lx_r, ld_s, ld_r, lf_s, lf_r,
    rring_s, rring_r, ra_s, ra_r, rd_s, rd_r, vs, vr, vfs, vfr, hs, hr, ts, tr,
):
    t, s = lax.axis_index("terms"), lax.axis_index("sectors")
    y, c = t // 2, lax.rem(t, 2)
    z, x = s // 4, lax.rem(s, 4)
    other = 1 - c
    ct = x // 2
    own = c == ct
    slot = jnp.where(own, lax.rem(x, 2), 2)
    same_row = lax.rem(x, 2)
    near_row = 1 - same_row
    outer = jnp.logical_or(x == 0, x == 3)
    near = jnp.where(outer != (c == 1), 1, -1)
    diag = y == z

    barrier = pltpu.get_barrier_semaphore()
    peers = [device(x, y, z, other)]
    for dx in (1, 2, 3):
        for e in (0, 1):
            peers.append(device(wrap(x + dx, X), y, z, e))
    for d in range(1, 8):
        peers.append(device(x, wrap(y + d, Y), z, c))
        peers.append(device(x, y, wrap(z + d, Z), c))
    for p in peers:
        pl.semaphore_signal(barrier, inc=1, device_id=p, device_id_type=MESH)
    pl.semaphore_wait(barrier, len(peers))

    sent = []

    def send(src, dst, ssem, rsem, to, when=None):
        cp = pltpu.make_async_remote_copy(
            src_ref=src, dst_ref=dst, send_sem=ssem, recv_sem=rsem, device_id=to, device_id_type=MESH
        )
        if when is None:
            cp.start()
        else:
            pl.when(when)(lambda: cp.start())
        sent.append((cp, when))

    def got(dst, rsem, when=None):
        cp = pltpu.make_async_remote_copy(
            src_ref=dst, dst_ref=dst, send_sem=rsem, recv_sem=rsem,
            device_id=device(x, y, z, other), device_id_type=MESH,
        )
        if when is None:
            cp.wait_recv()
        else:
            pl.when(when)(lambda: cp.wait_recv())

    yq = [wrap(y + o, Y) for o in OFFS]
    zq = [wrap(z + o, Z) for o in OFFS]
    wl = [4 * v + 2 * c for v in yq]

    def mine(q):
        return l_hbm if q == 0 else lb.at[slot, pl.ds(wl[q], 2)]

    def spread_l(q):
        src = mine(q)
        dst = lb.at[same_row, pl.ds(wl[q], 2)]
        for e, dx in enumerate((1, -1)):
            send(src, dst, lx_s.at[q, e], lx_r.at[q, c], device(wrap(x + dx, X), y, z, ct))
        send(src, dst, ld_s.at[q], ld_r.at[q], device(x, y, z, other), when=jnp.logical_not(own))

    def ring_l(q, up, to_q):
        src, w = mine(q), wl[q]
        to = device(x, wrap(y + (1 if up else -1), Y), z, c)
        if to_q < 7:
            send(src, lb.at[slot, pl.ds(w, 2)], lring_s.at[to_q], lring_r.at[to_q], to)
        else:
            i = 0 if up else 1
            send(lb.at[slot, w + i], lb.at[slot, w + i], lring_s.at[7 + i], lring_r.at[7 + i], to)

    def got_ring_l(q):
        if q < 7:
            got(lb.at[slot, pl.ds(wl[q], 2)], lring_r.at[q])
        else:
            for i in (0, 1):
                got(lb.at[slot, wl[q] + i], lring_r.at[7 + i])

    def piece_r(q):
        return r_hbm if q == 0 else rz.at[zq[q]]

    def ring_r(q, up, to_q):
        to = device(x, y, wrap(z + (1 if up else -1), Z), c)
        if to_q < 7:
            send(piece_r(q), rz.at[zq[q]], rring_s.at[to_q], rring_r.at[to_q], to)
        else:
            i = 0 if up else 1
            send(rz.at[zq[q], i], rz.at[zq[q], i], rring_s.at[7 + i], rring_r.at[7 + i], to)

    def got_ring_r(q):
        if q < 7:
            got(rz.at[zq[q]], rring_r.at[q])
        else:
            for i in (0, 1):
                got(rz.at[zq[q], i], rring_r.at[7 + i])

    w_own = 4 * y + 2 * c

    def spread_r(q):
        here = zq[q] == y
        send(
            piece_r(q), rb.at[pl.ds(w_own, 2)], ra_s.at[q], ra_r.at[y],
            device(x, zq[q], z, c), when=jnp.logical_not(here),
        )
        cp = pltpu.make_async_copy(piece_r(q), rb.at[pl.ds(w_own, 2)], local_sem.at[1])
        pl.when(here)(lambda: cp.start())

    ring_l(0, True, 1)
    ring_l(0, False, 2)
    ring_r(0, True, 1)
    ring_r(0, False, 2)
    send(v_hbm, vt.at[z], vs.at[0], vr.at[z], device(x, y, y, c), when=jnp.logical_not(diag))
    spread_l(0)
    spread_r(0)
    own_l = pltpu.make_async_copy(l_hbm, lb.at[slot, pl.ds(wl[0], 2)], local_sem.at[0])
    own_l.start()
    own_v = pltpu.make_async_copy(v_hbm, vc, local_sem.at[2])
    pl.when(diag)(lambda: own_v.start())

    def forward_near(q):
        for e in (0, 1):
            w = 4 * yq[q] + 2 * e
            got(lb.at[near_row, pl.ds(w, 2)], lx_r.at[q, e])
            j = jnp.where(near == -1, 0, 1)
            half = lb.at[near_row, w + j]
            send(half, half, lf_s.at[q, e], lf_r.at[q, e, j], device(wrap(x - near, X), y, z, c))

    nexts = {1: (True, 3), 2: (False, 4), 3: (True, 5), 4: (False, 6), 5: (True, 7), 6: (False, 7)}
    for q in range(1, 8):
        got_ring_l(q)
        if q in nexts:
            ring_l(q, *nexts[q])
        spread_l(q)
        got_ring_r(q)
        if q in nexts:
            ring_r(q, *nexts[q])
        spread_r(q)
        forward_near(q - 1)
        if q == 4:

            @pl.when(diag)
            def _():
                cps = []
                for d in range(1, 8):
                    zs = wrap(z + d, Z)
                    got(vt.at[zs], vr.at[zs])
                    cp = pltpu.make_async_remote_copy(
                        src_ref=vt.at[zs], dst_ref=vc, send_sem=vfs.at[d], recv_sem=vfr.at[0],
                        device_id=device(x, zs, z, c), device_id_type=MESH,
                    )
                    cp.start()
                    cps.append(cp)
                for cp in cps:
                    cp.wait_send()

    forward_near(7)
    own_l.wait()

    own_r = pltpu.make_async_copy(rz.at[0], rb.at[pl.ds(w_own, 2)], local_sem.at[1])
    own_r.wait()
    for d, o in enumerate(OFFS):
        ys = wrap(y + o, Y)
        ref = rb.at[pl.ds(4 * ys + 2 * c, 2)]
        if d:
            got(ref, ra_r.at[ys])
        send(ref, ref, rd_s.at[d], rd_r.at[ys], device(x, y, z, other))

    @pl.when(diag)
    def _():
        own_v.wait()

    got(vc, vfr.at[0], when=jnp.logical_not(diag))

    rows = lax.broadcasted_iota(jnp.int32, (BLK, BLK), 0)
    cols = lax.broadcasted_iota(jnp.int32, (BLK, BLK), 1)
    col_size = size_ref[4 * y + x]
    masks = [
        jnp.logical_and(rows < size_ref[4 * z + 2 * c + k], cols < col_size) for k in (0, 1)
    ]
    v = [
        jnp.where(masks[k], vc[pl.ds(BLK * k, BLK)].astype(jnp.float32), 0.0) for k in (0, 1)
    ]

    for q in range(8):
        got(lb.at[same_row, pl.ds(4 * yq[q] + 2 * other, 2)], ld_r.at[q], when=own)
        for e in (0, 1):
            for j in (0, 1):
                got(
                    lb.at[same_row, 4 * yq[q] + 2 * e + j], lf_r.at[q, e, j],
                    when=jnp.logical_not(own),
                )
    for d in range(8):
        ys = wrap(y + d, Y)
        got(rb.at[pl.ds(4 * ys + 2 * other, 2)], rd_r.at[ys])

    def apply(blocks):
        def left(i, carry):
            for k in (0, 1):
                a = lb[k, pl.ds(4 * i, 4)].reshape(4 * BLK, BLK)
                p = jnp.dot(a, blocks[k], preferred_element_type=jnp.float32)
                im[pl.ds(4 * i, 4), pl.ds(BLK * k, BLK)] = p.astype(jnp.bfloat16).reshape(4, BLK, BLK)
            return carry

        lax.fori_loop(0, 8, left, 0)

        def right(i, acc):
            a = jnp.concatenate([im[2 * i], im[2 * i + 1]], axis=1)
            b = jnp.concatenate([rb[2 * i], rb[2 * i + 1]], axis=1)
            return acc + lax.dot_general(
                a, b, (((1,), (1,)), ((), ())), preferred_element_type=jnp.float32
            )

        return lax.fori_loop(0, 16, right, jnp.zeros((2 * BLK, BLK), jnp.float32))

    total = apply([b.astype(jnp.bfloat16) for b in v])
    first = [jnp.where(masks[k], total[BLK * k : BLK * (k + 1)], 0.0) for k in (0, 1)]
    first_b = [f.astype(jnp.bfloat16).astype(jnp.float32) for f in first]

    def fold(a):
        return jnp.sum(a.reshape(BLK // 8, 8, BLK), axis=0)

    num = fold(v[0] * first_b[0]) + fold(v[1] * first_b[1])
    den = fold(v[0] * v[0]) + fold(v[1] * v[1])
    part[0, 0] = num
    part[0, 1] = den

    def swap(n, buf, devs):
        for i, to in enumerate(devs):
            send(part.at[n], buf.at[i], ts.at[8 * n + i], tr.at[8 * n + i], to)

    def add(n, buf, count):
        acc = part[n]
        for i in range(count):
            got(buf.at[i], tr.at[8 * n + i])
            acc = acc + buf[i]
        part[n + 1] = acc

    swap(0, core_in, [device(x, y, z, other)])

    num0, den0 = jnp.sum(num), jnp.sum(den)
    theta0 = jnp.where(den0 > 0.0, num0 / jnp.where(den0 > 0.0, den0, 1.0), 0.0)
    for k in (0, 1):
        s1[pl.ds(BLK * k, BLK)] = first[k]
    s1[pl.ds(2 * BLK, 8)] = jnp.full((8, BLK), theta0, jnp.float32)
    home = device(x, z, y, c)
    send(s1, s1h, hs.at[0], hr.at[0], home, when=jnp.logical_not(diag))
    home_s1 = pltpu.make_async_copy(s1, s1h, local_sem.at[3])
    pl.when(diag)(lambda: home_s1.start())

    add(0, core_in, 1)
    swap(1, x_in, [device(wrap(x + d, X), y, z, c) for d in (1, 2, 3)])

    corr = [(first_b[k] - theta0 * v[k]).astype(jnp.bfloat16) for k in (0, 1)]
    total2 = apply(corr)
    for k in (0, 1):
        g[pl.ds(BLK * k, BLK)] = jnp.where(masks[k], total2[BLK * k : BLK * (k + 1)], 0.0)
    send(g, gh, hs.at[1], hr.at[1], home, when=jnp.logical_not(diag))
    home_g = pltpu.make_async_copy(g, gh, local_sem.at[4])
    pl.when(diag)(lambda: home_g.start())

    add(1, x_in, 3)
    swap(2, y_in, [device(x, wrap(y + d, Y), z, c) for d in range(1, 8)])
    add(2, y_in, 7)
    swap(3, z_in, [device(x, y, wrap(z + d, Z), c) for d in range(1, 8)])

    got(s1h, hr.at[0], when=jnp.logical_not(diag))
    got(gh, hr.at[1], when=jnp.logical_not(diag))

    @pl.when(diag)
    def _():
        home_s1.wait()
        home_g.wait()

    out1[...] = s1h[pl.ds(0, 2 * BLK)].astype(jnp.bfloat16)
    add(3, z_in, 7)
    theta = jnp.sum(part[4, 0]) / jnp.sum(part[4, 1])
    shift = theta - s1h[2 * BLK, 0]
    home_col = size_ref[4 * z + x]
    for k in (0, 1):
        mask = jnp.logical_and(rows < size_ref[4 * y + 2 * c + k], cols < home_col)
        part_k = pl.ds(BLK * k, BLK)
        out2[part_k] = jnp.where(mask, gh[part_k] - shift * s1h[part_k], 0.0).astype(jnp.bfloat16)

    for cp, when in sent:
        if when is None:
            cp.wait_send()
        else:
            pl.when(when)(lambda cp=cp: cp.wait_send())


def shards(wavefunction, left_env, right_env, sector_size):
    left = left_env.reshape(2, BLK, BLK)
    right = right_env.reshape(2, BLK, BLK)
    bf, f32 = jnp.bfloat16, jnp.float32
    any_spec = pl.BlockSpec(memory_space=pl.ANY)
    vmem = pl.BlockSpec(memory_space=pltpu.VMEM)
    dma = pltpu.SemaphoreType.DMA
    out = jax.ShapeDtypeStruct((2 * BLK, BLK), bf)
    return pl.pallas_call(
        kernel,
        out_shape=(out, out),
        in_specs=[pl.BlockSpec(memory_space=pltpu.SMEM), any_spec, any_spec, any_spec],
        out_specs=(vmem, vmem),
        scratch_shapes=[
            pltpu.VMEM((3, 32, BLK, BLK), bf),
            pltpu.VMEM((Z, 2, BLK, BLK), bf),
            pltpu.VMEM((32, BLK, BLK), bf),
            pltpu.VMEM((Z, 2 * BLK, BLK), bf),
            pltpu.VMEM((2 * BLK, BLK), bf),
            pltpu.VMEM((32, 2 * BLK, BLK), bf),
            pltpu.VMEM((2 * BLK + 8, BLK), f32),
            pltpu.VMEM((2 * BLK, BLK), f32),
            pltpu.VMEM((2 * BLK + 8, BLK), f32),
            pltpu.VMEM((2 * BLK, BLK), f32),
            pltpu.VMEM((5, 2, 8, BLK), f32),
            pltpu.VMEM((1, 2, 8, BLK), f32),
            pltpu.VMEM((3, 2, 8, BLK), f32),
            pltpu.VMEM((7, 2, 8, BLK), f32),
            pltpu.VMEM((7, 2, 8, BLK), f32),
            dma((5,)),
            dma((9,)), dma((9,)), dma((8, 2)), dma((8, 2)), dma((8,)), dma((8,)), dma((8, 2)), dma((8, 2, 2)),
            dma((9,)), dma((9,)), dma((8,)), dma((8,)), dma((8,)), dma((8,)),
            dma((1,)), dma((8,)), dma((8,)), dma((1,)), dma((2,)), dma((2,)), dma((32,)), dma((32,)),
        ],
        compiler_params=pltpu.CompilerParams(
            collective_id=0, has_side_effects=True, vmem_limit_bytes=48 << 20
        ),
        name="davidson",
    )(sector_size, wavefunction, left, right)


def solution(mesh):
    return jax.shard_map(
        shards,
        mesh=mesh,
        in_specs=(
            P("terms", "sectors"),
            P("terms", "sectors", None, None),
            P("terms", "sectors", None, None),
            P(),
        ),
        out_specs=(P("terms", "sectors"), P("terms", "sectors")),
        check_vma=False,
    )
```

```python
import jax
import jax.numpy as jnp
from jax import lax
from jax.experimental import pallas as pl
from jax.experimental.pallas import tpu as pltpu
from jax.sharding import PartitionSpec as P

MESH = pl.DeviceIdType.MESH
BLK = 128
X, Y, Z = 4, 8, 8
OFFS = (0, -1, 1, -2, 2, -3, 3, 4)


def wrap(value, n):
    return lax.rem(value + 2 * n, n)


def device(x, y, z, c):
    return {"terms": 2 * y + c, "sectors": 4 * z + x}


def kernel(
    size_hbm, v_hbm, l_hbm, r_hbm, out1, out2,
    sizes, rb, ls, vc, im, s1, g, s1h, gh, part, x_in, y_in, z_in,
    local, ry_s, ry_r, rx_s, rx_r, rd_s, rd_r, rf_s, rf_r,
    lt_s, lt_r, lz_s, lz_r, ld_s, ld_r, v_s, v_r, h_s, h_r, t_s, t_r,
):
    t, s = lax.axis_index("terms"), lax.axis_index("sectors")
    y, c = t // 2, lax.rem(t, 2)
    z, x = s // 4, lax.rem(s, 4)
    other = 1 - c
    ct = x // 2
    own = c == ct
    odd = lax.rem(x, 2)
    slot = jnp.where(own, odd, 2)
    outer = jnp.logical_or(x == 0, x == 3)
    near = jnp.where(outer != (c == 1), 1, -1)
    diag = y == z
    off_diag = jnp.logical_not(diag)
    not_own = jnp.logical_not(own)

    barrier = pltpu.get_barrier_semaphore()
    peers = [device(x, y, z, other)]
    for d in (1, 2, 3):
        for e in (0, 1):
            peers.append(device(wrap(x + d, X), y, z, e))
    for d in range(1, 8):
        peers.append(device(x, wrap(y + d, Y), z, c))
        peers.append(device(x, y, wrap(z + d, Z), c))
    across = device(x, z, y, c)

    def hello(to):
        pl.semaphore_signal(barrier, inc=1, device_id=to, device_id_type=MESH)

    pl.when(off_diag)(lambda: hello(across))
    for p in peers:
        hello(p)

    def mine(ref):
        return lambda w: ref.at[pl.ds(w, 2)]

    get_sizes = pltpu.make_async_copy(size_hbm, sizes, local.at[0])
    get_sizes.start()
    own_r = pltpu.make_async_copy(r_hbm, rb.at[slot, pl.ds(4 * y + 2 * c, 2)], local.at[1])
    own_r.start()
    own_l = pltpu.make_async_copy(l_hbm, ls.at[pl.ds(4 * z + 2 * c, 2)], local.at[2])
    pl.when(diag)(lambda: own_l.start())
    own_v = pltpu.make_async_copy(v_hbm.at[pl.ds(BLK * odd, BLK)], vc.at[odd], local.at[3])
    pl.when(own)(lambda: own_v.start())

    pl.semaphore_wait(barrier, len(peers) + jnp.where(diag, 0, 1))

    sent = []

    def send(src, dst, ssem, rsem, to, when=None):
        cp = pltpu.make_async_remote_copy(
            src_ref=src, dst_ref=dst, send_sem=ssem, recv_sem=rsem, device_id=to, device_id_type=MESH
        )
        if when is None:
            cp.start()
        else:
            pl.when(when)(lambda: cp.start())
        sent.append((cp, when))

    def got(dst, rsem, when=None):
        cp = pltpu.make_async_remote_copy(
            src_ref=dst, dst_ref=dst, send_sem=rsem, recv_sem=rsem,
            device_id=device(x, y, z, other), device_id_type=MESH,
        )
        if when is None:
            cp.wait_recv()
        else:
            pl.when(when)(lambda: cp.wait_recv())

    yq = [wrap(y + o, Y) for o in OFFS]
    wr = [4 * v + 2 * c for v in yq]

    def piece_r(q):
        return r_hbm if q == 0 else rb.at[slot, pl.ds(wr[q], 2)]

    def pass_r(q, step, to_q):
        to = device(x, wrap(y + step, Y), z, c)
        if to_q < 7:
            send(piece_r(q), rb.at[slot, pl.ds(wr[q], 2)], ry_s.at[to_q], ry_r.at[to_q], to)
        else:
            i = 0 if step > 0 else 1
            half = rb.at[slot, wr[q] + i]
            send(half, half, ry_s.at[7 + i], ry_r.at[7 + i], to)

    def got_r(q):
        if q < 7:
            got(rb.at[slot, pl.ds(wr[q], 2)], ry_r.at[q])
        else:
            for i in (0, 1):
                got(rb.at[slot, wr[q] + i], ry_r.at[7 + i])

    def spread_r(q):
        dst = rb.at[odd, pl.ds(wr[q], 2)]
        for e, d in enumerate((1, -1)):
            send(piece_r(q), dst, rx_s.at[q, e], rx_r.at[q, c], device(wrap(x + d, X), y, z, ct))
        send(piece_r(q), dst, rd_s.at[q], rd_r.at[q], device(x, y, z, other), when=not_own)

    def beyond(q):
        for e in (0, 1):
            w = 4 * yq[q] + 2 * e
            got(rb.at[1 - odd, pl.ds(w, 2)], rx_r.at[q, e])
            j = jnp.where(near == -1, 0, 1)
            half = rb.at[1 - odd, w + j]
            send(half, half, rf_s.at[q, e], rf_r.at[q, e, j], device(wrap(x - near, X), y, z, c))

    def got_far(q):
        got(rb.at[odd, pl.ds(4 * yq[q] + 2 * other, 2)], rd_r.at[q], when=own)
        for e in (0, 1):
            for j in (0, 1):
                got(rb.at[odd, 4 * yq[q] + 2 * e + j], rf_r.at[q, e, j], when=not_own)

    zq = [wrap(z + o, Z) for o in OFFS]
    wz = [4 * v + 2 * c for v in zq]

    def pass_l(q, step, to_q):
        to = device(x, y, wrap(z + step, Z), c)
        if to_q < 7:
            ref = ls.at[pl.ds(wz[q], 2)]
            send(ref, ref, lz_s.at[to_q], lz_r.at[to_q], to)
        else:
            i = 0 if step > 0 else 1
            half = ls.at[wz[q] + i]
            send(half, half, lz_s.at[7 + i], lz_r.at[7 + i], to)

    def got_l(q):
        if q == 0:
            got(ls.at[pl.ds(wz[0], 2)], lt_r.at[0], when=off_diag)
            pl.when(diag)(lambda: own_l.wait())
        elif q < 7:
            got(ls.at[pl.ds(wz[q], 2)], lz_r.at[q])
        else:
            for i in (0, 1):
                got(ls.at[wz[q] + i], lz_r.at[7 + i])
        ref = ls.at[pl.ds(wz[q], 2)]
        send(ref, ref, ld_s.at[q], ld_r.at[q], device(x, y, z, other))

    def got_l_other(q):
        got(ls.at[pl.ds(4 * zq[q] + 2 * other, 2)], ld_r.at[q])

    relay = {1: (2, 5), 2: (-2, 6), 3: (2, 7), 4: (-2, 7)}
    first_steps = ((1, 1), (-1, 2), (2, 3), (-2, 4))

    send(l_hbm, ls.at[pl.ds(4 * y + 2 * c, 2)], lt_s.at[0], lt_r.at[0], across, when=off_diag)
    for step, to_q in first_steps:
        pass_r(0, step, to_q)
    spread_r(0)
    for k in (0, 1):
        keep = jnp.logical_and(own, odd == k)
        send(
            v_hbm.at[pl.ds(BLK * k, BLK)], vc.at[odd], v_s.at[k], v_r.at[odd],
            device(2 * c + k, y, z, ct), when=jnp.logical_not(keep),
        )

    def do_r(q):
        got_r(q)
        if q in relay:
            pass_r(q, *relay[q])
        spread_r(q)

    def do_l(q):
        got_l(q)
        if q in relay:
            pass_l(q, *relay[q])

    do_r(1)
    do_r(2)
    beyond(0)
    do_r(3)
    do_r(4)
    beyond(1)
    got_l(0)
    for step, to_q in first_steps:
        pass_l(0, step, to_q)
    beyond(2)
    do_r(5)
    do_r(6)
    do_r(7)
    beyond(3)
    beyond(4)
    do_l(1)
    do_l(2)
    beyond(5)
    do_l(3)
    do_l(4)
    beyond(6)
    beyond(7)

    get_sizes.wait()
    own_r.wait()
    pl.when(own)(lambda: own_v.wait())
    for k in (0, 1):
        keep = jnp.logical_and(own, odd == k)
        got(vc.at[k], v_r.at[k], when=jnp.logical_not(keep))
    rows = lax.broadcasted_iota(jnp.int32, (BLK, BLK), 0)
    cols = lax.broadcasted_iota(jnp.int32, (BLK, BLK), 1)
    row_live = rows < sizes[4 * y + x]
    masks = [jnp.logical_and(row_live, cols < sizes[4 * z + 2 * c + k]) for k in (0, 1)]
    v = [jnp.where(masks[k], vc[k].astype(jnp.float32), 0.0) for k in (0, 1)]

    def left(group, both):
        a = ls[pl.ds(4 * group, 4)].reshape(4 * BLK, BLK)
        p = jnp.dot(a, both, preferred_element_type=jnp.float32)
        im[pl.ds(4 * group, 4)] = p.astype(jnp.bfloat16).reshape(4, BLK, 2 * BLK)

    def right(group, acc):
        new = []
        for k in (0, 1):
            a = jnp.concatenate(
                [im[4 * group + i, :, pl.ds(BLK * k, BLK)] for i in range(4)], axis=1
            )
            b = jnp.concatenate([rb[k, 4 * group + i] for i in range(4)], axis=1)
            p = lax.dot_general(a, b, (((1,), (1,)), ((), ())), preferred_element_type=jnp.float32)
            new.append(acc[k] + p)
        return tuple(new)

    zero = (jnp.zeros((BLK, BLK), jnp.float32),) * 2
    both = jnp.concatenate([b.astype(jnp.bfloat16) for b in v], axis=1)
    for q in range(8):
        if q >= 5:
            got_l(q)
        got_l_other(q)
        left(zq[q], both)
    total = zero
    for q in range(8):
        got_far(q)
        total = right(yq[q], total)

    first = [jnp.where(masks[k], total[k], 0.0) for k in (0, 1)]
    first_b = [f.astype(jnp.bfloat16).astype(jnp.float32) for f in first]

    def fold(a):
        return jnp.sum(a.reshape(BLK // 8, 8, BLK), axis=0)

    num = fold(v[0] * first_b[0]) + fold(v[1] * first_b[1])
    den = fold(v[0] * v[0]) + fold(v[1] * v[1])
    part[0, 0] = num
    part[0, 1] = den

    def swap(n, buf, devs):
        for i, to in enumerate(devs):
            send(part.at[n], buf.at[i], t_s.at[8 * n + i], t_r.at[8 * n + i], to)

    def add(n, buf):
        acc = part[n]
        for i in range(7):
            got(buf.at[i], t_r.at[8 * n + i])
            acc = acc + buf[i]
        part[n + 1] = acc

    swap(0, x_in, [device(wrap(x + d // 2, X), y, z, wrap(c + d, 2)) for d in range(1, 8)])

    num0, den0 = jnp.sum(num), jnp.sum(den)
    theta0 = jnp.where(den0 > 0.0, num0 / jnp.where(den0 > 0.0, den0, 1.0), 0.0)

    def go_home(k, src, dst, n):
        keep = jnp.logical_and(own, odd == k)
        send(
            src.at[k], dst.at[odd], h_s.at[n, k], h_r.at[n, odd],
            device(2 * c + k, y, z, ct), when=jnp.logical_not(keep),
        )
        cp = pltpu.make_async_copy(src.at[k], dst.at[odd], local.at[4 + n])
        pl.when(keep)(lambda: cp.start())

    def got_home(dst, n):
        for k in (0, 1):
            keep = jnp.logical_and(own, odd == k)
            got(dst.at[k], h_r.at[n, k], when=jnp.logical_not(keep))
            cp = pltpu.make_async_copy(dst.at[k], dst.at[k], local.at[4 + n])
            pl.when(keep)(lambda: cp.wait())

    for k in (0, 1):
        s1[k, pl.ds(0, BLK)] = first[k]
        s1[k, pl.ds(BLK, 8)] = jnp.full((8, BLK), theta0, jnp.float32)
        go_home(k, s1, s1h, 0)

    corr = jnp.concatenate([(first_b[k] - theta0 * v[k]).astype(jnp.bfloat16) for k in (0, 1)], axis=1)

    def left_loop(i, carry):
        left(i, corr)
        return carry

    lax.fori_loop(0, 8, left_loop, 0)
    add(0, x_in)
    swap(1, y_in, [device(x, wrap(y + d, Y), z, c) for d in range(1, 8)])
    total2 = lax.fori_loop(0, 8, right, zero)
    for k in (0, 1):
        g[k] = jnp.where(masks[k], total2[k], 0.0)
        go_home(k, g, gh, 1)
    add(1, y_in)
    swap(2, z_in, [device(x, y, wrap(z + d, Z), c) for d in range(1, 8)])

    got_home(s1h, 0)
    got_home(gh, 1)
    for k in (0, 1):
        out1[pl.ds(BLK * k, BLK)] = s1h[k, pl.ds(0, BLK)].astype(jnp.bfloat16)
    for cp, when in sent:
        if when is None:
            cp.wait_send()
        else:
            pl.when(when)(lambda cp=cp: cp.wait_send())
    add(2, z_in)
    theta = jnp.sum(part[3, 0]) / jnp.sum(part[3, 1])
    home_live = cols < sizes[4 * z + x]
    for k in (0, 1):
        mask = jnp.logical_and(rows < sizes[4 * y + 2 * c + k], home_live)
        shift = theta - s1h[k, BLK, 0]
        new = gh[k] - shift * s1h[k, pl.ds(0, BLK)]
        out2[pl.ds(BLK * k, BLK)] = jnp.where(mask, new, 0.0).astype(jnp.bfloat16)


def shards(wavefunction, left_env, right_env, sector_size):
    left = left_env.reshape(2, BLK, BLK)
    right = right_env.reshape(2, BLK, BLK)
    bf, f32 = jnp.bfloat16, jnp.float32
    hbm = pl.BlockSpec(memory_space=pltpu.MemorySpace.HBM)
    vmem = pl.BlockSpec(memory_space=pltpu.VMEM)
    dma = pltpu.SemaphoreType.DMA
    out = jax.ShapeDtypeStruct((2 * BLK, BLK), bf)
    return pl.pallas_call(
        kernel,
        out_shape=(out, out),
        in_specs=[hbm, hbm, hbm, hbm],
        out_specs=(vmem, vmem),
        scratch_shapes=[
            pltpu.SMEM((32,), jnp.int32),
            pltpu.VMEM((3, 32, BLK, BLK), bf),
            pltpu.VMEM((32, BLK, BLK), bf),
            pltpu.VMEM((2, BLK, BLK), bf),
            pltpu.VMEM((32, BLK, 2 * BLK), bf),
            pltpu.VMEM((2, BLK + 8, BLK), f32),
            pltpu.VMEM((2, BLK, BLK), f32),
            pltpu.VMEM((2, BLK + 8, BLK), f32),
            pltpu.VMEM((2, BLK, BLK), f32),
            pltpu.VMEM((4, 2, 8, BLK), f32),
            pltpu.VMEM((7, 2, 8, BLK), f32),
            pltpu.VMEM((7, 2, 8, BLK), f32),
            pltpu.VMEM((7, 2, 8, BLK), f32),
            dma((6,)),
            dma((9,)), dma((9,)), dma((8, 2)), dma((8, 2)), dma((8,)), dma((8,)), dma((8, 2)), dma((8, 2, 2)),
            dma((1,)), dma((1,)), dma((9,)), dma((9,)), dma((8,)), dma((8,)),
            dma((2,)), dma((2,)), dma((2, 2)), dma((2, 2)), dma((24,)), dma((24,)),
        ],
        compiler_params=pltpu.CompilerParams(
            collective_id=0, has_side_effects=True, vmem_limit_bytes=48 << 20
        ),
        name="davidson",
    )(sector_size, wavefunction, left, right)


def solution(mesh):
    return jax.shard_map(
        shards,
        mesh=mesh,
        in_specs=(
            P("terms", "sectors"),
            P("terms", "sectors", None, None),
            P("terms", "sectors", None, None),
            P(),
        ),
        out_specs=(P("terms", "sectors"), P("terms", "sectors")),
        check_vma=False,
    )
```

```python
import jax
import jax.numpy as jnp
from jax import lax
from jax.experimental import pallas as pl
from jax.experimental.pallas import tpu as pltpu
from jax.sharding import PartitionSpec as P

MESH = pl.DeviceIdType.MESH
BLK = 128
X, Y, Z = 4, 8, 8
R_RELAY = {0: ((1, 1), (-1, 2)), 1: ((1, 3),), 2: ((-1, 4),), 3: ((1, 5),), 4: ((-1, 6),), 5: ((1, 7),), 6: ((-1, 7),)}
L_RELAY = {0: ((1, 1), (-1, 2), (2, 3), (-2, 4)), 1: ((2, 5),), 2: ((-2, 6),), 3: ((2, 7),), 4: ((-2, 7),)}
OFFS = (0, -1, 1, -2, 2, -3, 3, 4)


def wrap(value, n):
    return lax.rem(value + 2 * n, n)


def device(x, y, z, c):
    return {"terms": 2 * y + c, "sectors": 4 * z + x}


def kernel(
    size_hbm, v_hbm, l_hbm, r_hbm, out1, out2,
    sizes, v_own, l_own, rb, ls, vc, im, s1, g, s1h, gh, part, x_in, y_in, z_in,
    local, ry_s, ry_r, rx_s, rx_r, rd_s, rd_r,
    la_s, la_r, lz_s, lz_r, lx_s, lx_r, ld_s, ld_r, v_s, v_r, h_s, h_r, t_s, t_r,
):
    t, s = lax.axis_index("terms"), lax.axis_index("sectors")
    y, c = t // 2, lax.rem(t, 2)
    z, x = s // 4, lax.rem(s, 4)
    other = 1 - c
    xl, xr = x + 1 - 2 * lax.rem(x, 2), 3 - x
    lcore = lax.rem(x, 2)
    own_l = c == lcore
    not_own_l = jnp.logical_not(own_l)
    lslot = jnp.where(own_l, 0, 1)
    hcore = x // 2
    own_v = c == hcore
    diag = y == z
    off_diag = jnp.logical_not(diag)

    barrier = pltpu.get_barrier_semaphore()
    peers = [device(x, y, z, other)]
    for d in (1, 2, 3):
        for e in (0, 1):
            peers.append(device(wrap(x + d, X), y, z, e))
    for d in range(1, 8):
        peers.append(device(x, wrap(y + d, Y), z, c))
        peers.append(device(x, y, wrap(z + d, Z), c))
    across = device(x, z, y, c)

    def hello(to):
        pl.semaphore_signal(barrier, inc=1, device_id=to, device_id_type=MESH)

    pl.when(off_diag)(lambda: hello(across))
    for p in reversed(peers):
        hello(p)

    get_sizes = pltpu.make_async_copy(size_hbm, sizes, local.at[0])
    get_sizes.start()
    own_r = pltpu.make_async_copy(r_hbm, rb.at[0, pl.ds(4 * y + 2 * c, 2)], local.at[1])
    own_r.start()
    get_l = pltpu.make_async_copy(l_hbm, l_own, local.at[2])
    get_l.start()
    get_v = pltpu.make_async_copy(v_hbm, v_own, local.at[3])
    get_v.start()
    get_sizes.wait()
    own_r.wait()
    get_l.wait()
    get_v.wait()
    pl.semaphore_wait(barrier, len(peers) + jnp.where(diag, 0, 1))

    sent = []

    def send(src, dst, ssem, rsem, to, when=None):
        cp = pltpu.make_async_remote_copy(
            src_ref=src, dst_ref=dst, send_sem=ssem, recv_sem=rsem, device_id=to, device_id_type=MESH
        )
        if when is None:
            cp.start()
        else:
            pl.when(when)(lambda: cp.start())
        sent.append((cp, when))

    def got(dst, rsem, when=None):
        cp = pltpu.make_async_remote_copy(
            src_ref=dst, dst_ref=dst, send_sem=rsem, recv_sem=rsem,
            device_id=device(x, y, z, other), device_id_type=MESH,
        )
        if when is None:
            cp.wait_recv()
        else:
            pl.when(when)(lambda: cp.wait_recv())

    yq = [wrap(y + o, Y) for o in OFFS]
    wr = [4 * v + 2 * c for v in yq]
    wo = [4 * v + 2 * other for v in yq]
    sibling = device(x, y, z, other)

    def pass_r(q, step, to_q):
        to = device(x, wrap(y + step, Y), z, c)
        if to_q < 7:
            ref = rb.at[0, pl.ds(wr[q], 2)]
            send(ref, ref, ry_s.at[to_q], ry_r.at[to_q], to)
        else:
            i = 0 if step > 0 else 1
            half = rb.at[0, wr[q] + i]
            send(half, half, ry_s.at[7 + i], ry_r.at[7 + i], to)

    def got_r(q):
        if q < 7:
            got(rb.at[0, pl.ds(wr[q], 2)], ry_r.at[q])
        else:
            for i in (0, 1):
                got(rb.at[0, wr[q] + i], ry_r.at[7 + i])

    def spread_r(q):
        ref = rb.at[0, pl.ds(wr[q], 2)]
        send(ref, rb.at[1, pl.ds(wr[q], 2)], rx_s.at[q], rx_r.at[q], device(xr, y, z, c))
        send(ref, ref, rd_s.at[0, q], rd_r.at[0, q], sibling)

    def beyond(q):
        ref = rb.at[1, pl.ds(wr[q], 2)]
        got(ref, rx_r.at[q])
        send(ref, ref, rd_s.at[1, q], rd_r.at[1, q], sibling)

    def got_far(q):
        for k in (0, 1):
            got(rb.at[k, pl.ds(wo[q], 2)], rd_r.at[k, q])

    zq = [wrap(z + o, Z) for o in OFFS]
    wz = [4 * v + 2 * c for v in zq]
    wzo = [4 * v + 2 * other for v in zq]

    def start_l():
        dst = ls.at[lslot, pl.ds(4 * y + 2 * c, 2)]
        send(l_own, dst, la_s.at[0], la_r.at[0], across, when=off_diag)
        cp = pltpu.make_async_copy(l_own, dst, local.at[2])
        pl.when(diag)(lambda: cp.start())

    def pass_l(q, step, to_q):
        to = device(x, y, wrap(z + step, Z), c)
        if to_q < 7:
            ref = ls.at[lslot, pl.ds(wz[q], 2)]
            send(ref, ref, lz_s.at[to_q], lz_r.at[to_q], to)
        else:
            i = 0 if step > 0 else 1
            half = ls.at[lslot, wz[q] + i]
            send(half, half, lz_s.at[7 + i], lz_r.at[7 + i], to)

    def got_l(q):
        ref = ls.at[lslot, pl.ds(wz[q], 2)]
        if q == 0:
            cp = pltpu.make_async_copy(l_own, ref, local.at[2])
            pl.when(diag)(lambda: cp.wait())
            got(ref, la_r.at[0], when=off_diag)
        elif q < 7:
            got(ref, lz_r.at[q])
        else:
            for i in (0, 1):
                got(ls.at[lslot, wz[q] + i], lz_r.at[7 + i])

    def do_l(q):
        got_l(q)
        for step, to_q in L_RELAY.get(q, ()):
            pass_l(q, step, to_q)
        ref = ls.at[lslot, pl.ds(wz[q], 2)]
        dst = ls.at[0, pl.ds(wz[q], 2)]
        send(ref, dst, lx_s.at[q], lx_r.at[q, c], device(xl, y, z, lcore))
        send(ref, dst, ld_s.at[q], ld_r.at[q], sibling, when=not_own_l)

    def got_l_other(q):
        got(ls.at[0, pl.ds(wzo[q], 2)], ld_r.at[q], when=own_l)
        for e in (0, 1):
            got(ls.at[0, pl.ds(4 * zq[q] + 2 * e, 2)], lx_r.at[q, e], when=not_own_l)

    def do_r(q):
        got_r(q)
        for step, to_q in R_RELAY.get(q, ()):
            pass_r(q, step, to_q)
        spread_r(q)

    start_l()
    for step, to_q in R_RELAY[0]:
        pass_r(0, step, to_q)
    spread_r(0)
    v_chip = jnp.where(own_v, x, xr)
    v_slot = jnp.where(own_v, 0, 1)
    for k in (0, 1):
        keep = jnp.logical_and(own_v, c == k)
        src = v_own.at[pl.ds(BLK * k, BLK)]
        send(
            src, vc.at[v_slot], v_s.at[k], v_r.at[v_slot],
            device(v_chip, y, z, k), when=jnp.logical_not(keep),
        )
        cp = pltpu.make_async_copy(src, vc.at[0], local.at[3])
        pl.when(keep)(lambda: cp.start())
    do_r(1)
    do_r(2)
    beyond(0)
    do_r(3)
    do_r(4)
    beyond(1)
    beyond(2)
    do_l(0)
    do_r(5)
    do_r(6)
    beyond(3)
    beyond(4)
    do_r(7)
    beyond(5)
    beyond(6)
    do_l(1)
    do_l(2)
    do_l(3)
    do_l(4)
    beyond(7)
    do_l(5)
    do_l(6)
    do_l(7)

    got(vc.at[0], v_r.at[0], when=jnp.logical_not(own_v))
    own_block = pltpu.make_async_copy(vc.at[0], vc.at[0], local.at[3])
    pl.when(own_v)(lambda: own_block.wait())
    got(vc.at[1], v_r.at[1])
    rows = lax.broadcasted_iota(jnp.int32, (BLK, BLK), 0)
    cols = lax.broadcasted_iota(jnp.int32, (BLK, BLK), 1)
    row_live = rows < sizes[4 * y + 2 * hcore + c]
    masks = [jnp.logical_and(row_live, cols < sizes[4 * z + n]) for n in (x, xr)]
    v = [jnp.where(masks[k], vc[k].astype(jnp.float32), 0.0) for k in (0, 1)]

    def left(group, both):
        a = ls[0, pl.ds(4 * group, 4)].reshape(4 * BLK, BLK)
        p = jnp.dot(a, both, preferred_element_type=jnp.float32)
        im[pl.ds(4 * group, 4)] = p.astype(jnp.bfloat16).reshape(4, BLK, 2 * BLK)

    def right(group, acc):
        new = []
        for k in (0, 1):
            a = jnp.concatenate(
                [im[4 * group + i, :, pl.ds(BLK * k, BLK)] for i in range(4)], axis=1
            )
            b = jnp.concatenate([rb[k, 4 * group + i] for i in range(4)], axis=1)
            p = lax.dot_general(a, b, (((1,), (1,)), ((), ())), preferred_element_type=jnp.float32)
            new.append(acc[k] + p)
        return tuple(new)

    zero = (jnp.zeros((BLK, BLK), jnp.float32),) * 2
    both = jnp.concatenate([b.astype(jnp.bfloat16) for b in v], axis=1)
    for q in range(5):
        got_l_other(q)
        left(zq[q], both)
    for q in range(8):
        got_far(q)
    total = zero
    for q in range(5):
        total = right(zq[q], total)
    for q in range(5, 8):
        got_l_other(q)
        left(zq[q], both)
        total = right(zq[q], total)

    first = [jnp.where(masks[k], total[k], 0.0) for k in (0, 1)]
    first_b = [f.astype(jnp.bfloat16).astype(jnp.float32) for f in first]

    def fold(a):
        return jnp.sum(a.reshape(BLK // 8, 8, BLK), axis=0)

    def fold_more(a):
        return a[:4] + a[4:]

    num = fold_more(fold(v[0] * first_b[0]) + fold(v[1] * first_b[1]))
    den = fold_more(fold(v[0] * v[0]) + fold(v[1] * v[1]))
    part[0] = jnp.concatenate([num, den], axis=0)

    def swap(n, buf, devs):
        for i, to in enumerate(devs):
            send(part.at[n], buf.at[i], t_s.at[8 * n + i], t_r.at[8 * n + i], to)

    def add(n, buf):
        acc = part[n]
        for i in range(7):
            got(buf.at[i], t_r.at[8 * n + i])
            acc = acc + buf[i]
        part[n + 1] = acc

    swap(0, x_in, [device(wrap(x + d // 2, X), y, z, wrap(c + d, 2)) for d in range(1, 8)])

    num0, den0 = jnp.sum(num), jnp.sum(den)
    theta0 = jnp.where(den0 > 0.0, num0 / jnp.where(den0 > 0.0, den0, 1.0), 0.0)

    def go_home(k, src, dst, n):
        to = device((x, xr)[k], y, z, hcore)
        if k == 0:
            send(src.at[0], dst.at[c], h_s.at[n, 0], h_r.at[n, c], to, when=jnp.logical_not(own_v))
            cp = pltpu.make_async_copy(src.at[0], dst.at[c], local.at[4 + n])
            pl.when(own_v)(lambda: cp.start())
        else:
            send(src.at[1], dst.at[c], h_s.at[n, 1], h_r.at[n, c], to)

    def got_home(dst, n):
        for k in (0, 1):
            keep = jnp.logical_and(own_v, c == k)
            got(dst.at[k], h_r.at[n, k], when=jnp.logical_not(keep))
            cp = pltpu.make_async_copy(dst.at[k], dst.at[k], local.at[4 + n])
            pl.when(keep)(lambda: cp.wait())

    for k in (0, 1):
        s1[k, pl.ds(0, BLK)] = first[k]
        s1[k, pl.ds(BLK, 8)] = jnp.full((8, BLK), theta0, jnp.float32)
        go_home(k, s1, s1h, 0)

    corr = jnp.concatenate([(first_b[k] - theta0 * v[k]).astype(jnp.bfloat16) for k in (0, 1)], axis=1)

    def left_loop(i, carry):
        left(i, corr)
        return carry

    lax.fori_loop(0, 8, left_loop, 0)
    add(0, x_in)
    swap(1, y_in, [device(x, wrap(y + d, Y), z, c) for d in (4, 3, 5, 2, 6, 1, 7)])
    total2 = lax.fori_loop(0, 8, right, zero)
    for k in (0, 1):
        g[k] = jnp.where(masks[k], total2[k], 0.0)
        go_home(k, g, gh, 1)
    add(1, y_in)
    swap(2, z_in, [device(x, y, wrap(z + d, Z), c) for d in (4, 3, 5, 2, 6, 1, 7)])

    got_home(s1h, 0)
    got_home(gh, 1)
    for k in (0, 1):
        out1[pl.ds(BLK * k, BLK)] = s1h[k, pl.ds(0, BLK)].astype(jnp.bfloat16)
    for cp, when in sent:
        if when is None:
            cp.wait_send()
        else:
            pl.when(when)(lambda cp=cp: cp.wait_send())
    add(2, z_in)
    theta = jnp.sum(part[3, pl.ds(0, 4)]) / jnp.sum(part[3, pl.ds(4, 4)])
    home_live = cols < sizes[4 * z + x]
    for k in (0, 1):
        mask = jnp.logical_and(rows < sizes[4 * y + 2 * c + k], home_live)
        shift = theta - s1h[k, BLK, 0]
        new = gh[k] - shift * s1h[k, pl.ds(0, BLK)]
        out2[pl.ds(BLK * k, BLK)] = jnp.where(mask, new, 0.0).astype(jnp.bfloat16)


def shards(wavefunction, left_env, right_env, sector_size):
    left = left_env.reshape(2, BLK, BLK)
    right = right_env.reshape(2, BLK, BLK)
    bf, f32 = jnp.bfloat16, jnp.float32
    hbm = pl.BlockSpec(memory_space=pltpu.MemorySpace.HBM)
    vmem = pl.BlockSpec(memory_space=pltpu.VMEM)
    dma = pltpu.SemaphoreType.DMA
    out = jax.ShapeDtypeStruct((2 * BLK, BLK), bf)
    return pl.pallas_call(
        kernel,
        out_shape=(out, out),
        in_specs=[hbm, hbm, hbm, hbm],
        out_specs=(vmem, vmem),
        scratch_shapes=[
            pltpu.SMEM((32,), jnp.int32),
            pltpu.VMEM((2 * BLK, BLK), bf),
            pltpu.VMEM((2, BLK, BLK), bf),
            pltpu.VMEM((2, 32, BLK, BLK), bf),
            pltpu.VMEM((2, 32, BLK, BLK), bf),
            pltpu.VMEM((2, BLK, BLK), bf),
            pltpu.VMEM((32, BLK, 2 * BLK), bf),
            pltpu.VMEM((2, BLK + 8, BLK), f32),
            pltpu.VMEM((2, BLK, BLK), f32),
            pltpu.VMEM((2, BLK + 8, BLK), f32),
            pltpu.VMEM((2, BLK, BLK), f32),
            pltpu.VMEM((4, 8, BLK), f32),
            pltpu.VMEM((7, 8, BLK), f32),
            pltpu.VMEM((7, 8, BLK), f32),
            pltpu.VMEM((7, 8, BLK), f32),
            dma((6,)),
            dma((9,)), dma((9,)), dma((8,)), dma((8,)), dma((2, 8)), dma((2, 8)),
            dma((1,)), dma((1,)), dma((9,)), dma((9,)), dma((8,)), dma((8, 2)), dma((8,)), dma((8,)),
            dma((2,)), dma((2,)), dma((2, 2)), dma((2, 2)), dma((24,)), dma((24,)),
        ],
        compiler_params=pltpu.CompilerParams(
            collective_id=0, has_side_effects=True, vmem_limit_bytes=60 << 20
        ),
        name="davidson",
    )(sector_size, wavefunction, left, right)


def solution(mesh):
    return jax.shard_map(
        shards,
        mesh=mesh,
        in_specs=(
            P("terms", "sectors"),
            P("terms", "sectors", None, None),
            P("terms", "sectors", None, None),
            P(),
        ),
        out_specs=(P("terms", "sectors"), P("terms", "sectors")),
        check_vma=False,
    )
```

```python
import jax
import jax.numpy as jnp
from jax import lax
from jax.experimental import pallas as pl
from jax.experimental.pallas import tpu as pltpu
from jax.sharding import PartitionSpec as P

MESH = pl.DeviceIdType.MESH
BLK = 128
X, Y, Z = 4, 8, 8
R_RELAY = {0: ((1, 1), (-1, 2)), 1: ((1, 3),), 2: ((-1, 4),), 3: ((1, 5),), 4: ((-1, 6),), 5: ((1, 7),), 6: ((-1, 7),)}
L_RELAY = {0: ((1, 1), (-1, 2), (2, 3), (-2, 4)), 1: ((2, 5),), 2: ((-2, 6),), 3: ((2, 7),), 4: ((-2, 7),)}
OFFS = (0, -1, 1, -2, 2, -3, 3, 4)


def wrap(value, n):
    return lax.rem(value + 2 * n, n)


def device(x, y, z, c):
    return {"terms": 2 * y + c, "sectors": 4 * z + x}


def kernel(
    size_hbm, v_hbm, l_hbm, r_hbm, out,
    sizes, v_own, l_own, rb, ls, vc, im, s1, g, s1h, gh, part, x_in, y_in, z_in,
    local, ry_s, ry_r, rx_s, rx_r, rd_s, rd_r,
    la_s, la_r, lz_s, lz_r, lx_s, lx_r, ld_s, ld_r, v_s, v_r, h_s, h_r, t_s, t_r,
):
    t, s = lax.axis_index("terms"), lax.axis_index("sectors")
    y, c = t // 2, lax.rem(t, 2)
    z, x = s // 4, lax.rem(s, 4)
    other = 1 - c
    xl, xr = x + 1 - 2 * lax.rem(x, 2), 3 - x
    lcore = lax.rem(x, 2)
    own_l = c == lcore
    not_own_l = jnp.logical_not(own_l)
    lslot = jnp.where(own_l, 0, 1)
    hcore = x // 2
    own_v = c == hcore
    diag = y == z
    off_diag = jnp.logical_not(diag)

    barrier = pltpu.get_barrier_semaphore()
    peers = [device(x, y, z, other)]
    for d in (1, 2, 3):
        for e in (0, 1):
            peers.append(device(wrap(x + d, X), y, z, e))
    for d in range(1, 8):
        peers.append(device(x, wrap(y + d, Y), z, c))
        peers.append(device(x, y, wrap(z + d, Z), c))
    across = device(x, z, y, c)

    def hello(to):
        pl.semaphore_signal(barrier, inc=1, device_id=to, device_id_type=MESH)

    pl.when(off_diag)(lambda: hello(across))
    for p in reversed(peers):
        hello(p)

    get_sizes = pltpu.make_async_copy(size_hbm, sizes, local.at[0])
    get_sizes.start()
    own_r = pltpu.make_async_copy(r_hbm, rb.at[0, pl.ds(4 * y + 2 * c, 2)], local.at[1])
    own_r.start()
    get_l = pltpu.make_async_copy(l_hbm, l_own, local.at[2])
    get_l.start()
    get_v = pltpu.make_async_copy(v_hbm, v_own, local.at[3])
    get_v.start()
    get_sizes.wait()
    own_r.wait()
    get_l.wait()
    get_v.wait()
    pl.semaphore_wait(barrier, len(peers) + jnp.where(diag, 0, 1))

    sent = []

    def send(src, dst, ssem, rsem, to, when=None):
        cp = pltpu.make_async_remote_copy(
            src_ref=src, dst_ref=dst, send_sem=ssem, recv_sem=rsem, device_id=to, device_id_type=MESH
        )
        if when is None:
            cp.start()
        else:
            pl.when(when)(lambda: cp.start())
        sent.append((cp, when))

    def got(dst, rsem, when=None):
        cp = pltpu.make_async_remote_copy(
            src_ref=dst, dst_ref=dst, send_sem=rsem, recv_sem=rsem,
            device_id=device(x, y, z, other), device_id_type=MESH,
        )
        if when is None:
            cp.wait_recv()
        else:
            pl.when(when)(lambda: cp.wait_recv())

    yq = [wrap(y + o, Y) for o in OFFS]
    wr = [4 * v + 2 * c for v in yq]
    wo = [4 * v + 2 * other for v in yq]
    sibling = device(x, y, z, other)

    def pass_r(q, step, to_q):
        to = device(x, wrap(y + step, Y), z, c)
        if to_q < 7:
            ref = rb.at[0, pl.ds(wr[q], 2)]
            send(ref, ref, ry_s.at[to_q], ry_r.at[to_q], to)
        else:
            i = 0 if step > 0 else 1
            half = rb.at[0, wr[q] + i]
            send(half, half, ry_s.at[7 + i], ry_r.at[7 + i], to)

    def got_r(q):
        if q < 7:
            got(rb.at[0, pl.ds(wr[q], 2)], ry_r.at[q])
        else:
            for i in (0, 1):
                got(rb.at[0, wr[q] + i], ry_r.at[7 + i])

    def spread_r(q):
        ref = rb.at[0, pl.ds(wr[q], 2)]
        send(ref, rb.at[1, pl.ds(wr[q], 2)], rx_s.at[q], rx_r.at[q], device(xr, y, z, c))
        send(ref, ref, rd_s.at[0, q], rd_r.at[0, q], sibling)

    def beyond(q):
        ref = rb.at[1, pl.ds(wr[q], 2)]
        got(ref, rx_r.at[q])
        send(ref, ref, rd_s.at[1, q], rd_r.at[1, q], sibling)

    def got_far(q):
        for k in (0, 1):
            got(rb.at[k, pl.ds(wo[q], 2)], rd_r.at[k, q])

    zq = [wrap(z + o, Z) for o in OFFS]
    wz = [4 * v + 2 * c for v in zq]
    wzo = [4 * v + 2 * other for v in zq]

    def start_l():
        dst = ls.at[lslot, pl.ds(4 * y + 2 * c, 2)]
        send(l_own, dst, la_s.at[0], la_r.at[0], across, when=off_diag)
        cp = pltpu.make_async_copy(l_own, dst, local.at[2])
        pl.when(diag)(lambda: cp.start())

    def pass_l(q, step, to_q):
        to = device(x, y, wrap(z + step, Z), c)
        if to_q < 7:
            ref = ls.at[lslot, pl.ds(wz[q], 2)]
            send(ref, ref, lz_s.at[to_q], lz_r.at[to_q], to)
        else:
            i = 0 if step > 0 else 1
            half = ls.at[lslot, wz[q] + i]
            send(half, half, lz_s.at[7 + i], lz_r.at[7 + i], to)

    def got_l(q):
        ref = ls.at[lslot, pl.ds(wz[q], 2)]
        if q == 0:
            cp = pltpu.make_async_copy(l_own, ref, local.at[2])
            pl.when(diag)(lambda: cp.wait())
            got(ref, la_r.at[0], when=off_diag)
        elif q < 7:
            got(ref, lz_r.at[q])
        else:
            for i in (0, 1):
                got(ls.at[lslot, wz[q] + i], lz_r.at[7 + i])

    def do_l(q):
        got_l(q)
        for step, to_q in L_RELAY.get(q, ()):
            pass_l(q, step, to_q)
        ref = ls.at[lslot, pl.ds(wz[q], 2)]
        dst = ls.at[0, pl.ds(wz[q], 2)]
        send(ref, dst, lx_s.at[q], lx_r.at[q, c], device(xl, y, z, lcore))
        send(ref, dst, ld_s.at[q], ld_r.at[q], sibling, when=not_own_l)

    def got_l_other(q):
        got(ls.at[0, pl.ds(wzo[q], 2)], ld_r.at[q], when=own_l)
        for e in (0, 1):
            got(ls.at[0, pl.ds(4 * zq[q] + 2 * e, 2)], lx_r.at[q, e], when=not_own_l)

    def do_r(q):
        got_r(q)
        for step, to_q in R_RELAY.get(q, ()):
            pass_r(q, step, to_q)
        spread_r(q)

    start_l()
    for step, to_q in R_RELAY[0]:
        pass_r(0, step, to_q)
    spread_r(0)
    v_chip = jnp.where(own_v, x, xr)
    v_slot = jnp.where(own_v, 0, 1)
    for k in (0, 1):
        keep = jnp.logical_and(own_v, c == k)
        src = v_own.at[pl.ds(BLK * k, BLK)]
        send(
            src, vc.at[v_slot], v_s.at[k], v_r.at[v_slot],
            device(v_chip, y, z, k), when=jnp.logical_not(keep),
        )
        cp = pltpu.make_async_copy(src, vc.at[0], local.at[3])
        pl.when(keep)(lambda: cp.start())
    do_r(1)
    do_r(2)
    beyond(0)
    do_l(0)
    do_r(3)
    do_r(4)
    beyond(1)
    beyond(2)
    do_r(5)
    do_r(6)
    beyond(3)
    beyond(4)
    do_l(1)
    do_l(2)
    do_r(7)
    do_l(3)
    do_l(4)
    beyond(5)
    beyond(6)
    beyond(7)
    do_l(5)
    do_l(6)
    do_l(7)

    got(vc.at[0], v_r.at[0], when=jnp.logical_not(own_v))
    own_block = pltpu.make_async_copy(vc.at[0], vc.at[0], local.at[3])
    pl.when(own_v)(lambda: own_block.wait())
    got(vc.at[1], v_r.at[1])
    rows = lax.broadcasted_iota(jnp.int32, (BLK, BLK), 0)
    cols = lax.broadcasted_iota(jnp.int32, (BLK, BLK), 1)
    row_live = rows < sizes[4 * y + 2 * hcore + c]
    masks = [jnp.logical_and(row_live, cols < sizes[4 * z + n]) for n in (x, xr)]
    v = [jnp.where(masks[k], vc[k].astype(jnp.float32), 0.0) for k in (0, 1)]

    def left(group, both):
        a = ls[0, pl.ds(4 * group, 4)].reshape(4 * BLK, BLK)
        p = jnp.dot(a, both, preferred_element_type=jnp.float32)
        im[pl.ds(4 * group, 4)] = p.astype(jnp.bfloat16).reshape(4, BLK, 2 * BLK)

    def right(group, acc):
        new = []
        for k in (0, 1):
            a = jnp.concatenate(
                [im[4 * group + i, :, pl.ds(BLK * k, BLK)] for i in range(4)], axis=1
            )
            b = jnp.concatenate([rb[k, 4 * group + i] for i in range(4)], axis=1)
            p = lax.dot_general(a, b, (((1,), (1,)), ((), ())), preferred_element_type=jnp.float32)
            new.append(acc[k] + p)
        return tuple(new)

    zero = (jnp.zeros((BLK, BLK), jnp.float32),) * 2
    both = jnp.concatenate([b.astype(jnp.bfloat16) for b in v], axis=1)
    for q in range(5):
        got_l_other(q)
        left(zq[q], both)
    for q in range(8):
        got_far(q)
    total = zero
    for q in range(5):
        total = right(zq[q], total)
    for q in range(5, 8):
        got_l_other(q)
        left(zq[q], both)
        total = right(zq[q], total)

    first = [jnp.where(masks[k], total[k], 0.0) for k in (0, 1)]
    first_b = [f.astype(jnp.bfloat16).astype(jnp.float32) for f in first]

    def fold(a):
        return jnp.sum(a.reshape(BLK // 8, 8, BLK), axis=0)

    def fold_more(a):
        return a[:4] + a[4:]

    num = fold_more(fold(v[0] * first_b[0]) + fold(v[1] * first_b[1]))
    den = fold_more(fold(v[0] * v[0]) + fold(v[1] * v[1]))
    part[0] = jnp.concatenate([num, den], axis=0)

    def swap(n, buf, devs):
        for i, to in enumerate(devs):
            send(part.at[n], buf.at[i], t_s.at[8 * n + i], t_r.at[8 * n + i], to)

    def add(n, buf):
        acc = part[n]
        for i in range(7):
            got(buf.at[i], t_r.at[8 * n + i])
            acc = acc + buf[i]
        part[n + 1] = acc

    swap(0, x_in, [device(wrap(x + d // 2, X), y, z, wrap(c + d, 2)) for d in range(1, 8)])

    num0, den0 = jnp.sum(num), jnp.sum(den)
    theta0 = jnp.where(den0 > 0.0, num0 / jnp.where(den0 > 0.0, den0, 1.0), 0.0)

    def go_home(k, src, dst, n):
        to = device((x, xr)[k], y, z, hcore)
        if k == 0:
            send(src.at[0], dst.at[c], h_s.at[n, 0], h_r.at[n, c], to, when=jnp.logical_not(own_v))
            cp = pltpu.make_async_copy(src.at[0], dst.at[c], local.at[4 + n])
            pl.when(own_v)(lambda: cp.start())
        else:
            send(src.at[1], dst.at[c], h_s.at[n, 1], h_r.at[n, c], to)

    def got_home(dst, n):
        for k in (0, 1):
            keep = jnp.logical_and(own_v, c == k)
            got(dst.at[k], h_r.at[n, k], when=jnp.logical_not(keep))
            cp = pltpu.make_async_copy(dst.at[k], dst.at[k], local.at[4 + n])
            pl.when(keep)(lambda: cp.wait())

    for k in (0, 1):
        s1[k, pl.ds(0, BLK)] = first[k]
        s1[k, pl.ds(BLK, 8)] = jnp.full((8, BLK), theta0, jnp.float32)
        go_home(k, s1, s1h, 0)

    corr = jnp.concatenate([(first_b[k] - theta0 * v[k]).astype(jnp.bfloat16) for k in (0, 1)], axis=1)

    def left_loop(i, carry):
        left(i, corr)
        return carry

    lax.fori_loop(0, 8, left_loop, 0)
    add(0, x_in)
    swap(1, y_in, [device(x, wrap(y + d, Y), z, c) for d in (4, 3, 5, 2, 6, 1, 7)])
    total2 = lax.fori_loop(0, 8, right, zero)
    for k in (0, 1):
        g[k] = jnp.where(masks[k], total2[k], 0.0)
        go_home(k, g, gh, 1)
    add(1, y_in)
    swap(2, z_in, [device(x, y, wrap(z + d, Z), c) for d in (4, 3, 5, 2, 6, 1, 7)])

    got_home(s1h, 0)
    got_home(gh, 1)
    for k in (0, 1):
        out[pl.ds(BLK * k, BLK)] = s1h[k, pl.ds(0, BLK)]
    for cp, when in sent:
        if when is None:
            cp.wait_send()
        else:
            pl.when(when)(lambda cp=cp: cp.wait_send())
    add(2, z_in)
    sums = part[3]
    theta = jnp.sum(sums[:4], keepdims=True) / jnp.sum(sums[4:], keepdims=True)
    home_live = cols < sizes[4 * z + x]
    for k in (0, 1):
        mask = jnp.logical_and(rows < sizes[4 * y + 2 * c + k], home_live)
        shift = theta - s1h[k, pl.ds(BLK, 1)]
        new = gh[k] - shift * s1h[k, pl.ds(0, BLK)]
        out[pl.ds(BLK * (k + 2), BLK)] = jnp.where(mask, new, 0.0)


def shards(wavefunction, left_env, right_env, sector_size):
    left = left_env.reshape(2, BLK, BLK)
    right = right_env.reshape(2, BLK, BLK)
    bf, f32 = jnp.bfloat16, jnp.float32
    hbm = pl.BlockSpec(memory_space=pltpu.MemorySpace.HBM)
    vmem = pl.BlockSpec(memory_space=pltpu.VMEM)
    dma = pltpu.SemaphoreType.DMA
    wide = pl.pallas_call(
        kernel,
        out_shape=jax.ShapeDtypeStruct((4 * BLK, BLK), f32),
        in_specs=[hbm, hbm, hbm, hbm],
        out_specs=vmem,
        scratch_shapes=[
            pltpu.SMEM((32,), jnp.int32),
            pltpu.VMEM((2 * BLK, BLK), bf),
            pltpu.VMEM((2, BLK, BLK), bf),
            pltpu.VMEM((2, 32, BLK, BLK), bf),
            pltpu.VMEM((2, 32, BLK, BLK), bf),
            pltpu.VMEM((2, BLK, BLK), bf),
            pltpu.VMEM((32, BLK, 2 * BLK), bf),
            pltpu.VMEM((2, BLK + 8, BLK), f32),
            pltpu.VMEM((2, BLK, BLK), f32),
            pltpu.VMEM((2, BLK + 8, BLK), f32),
            pltpu.VMEM((2, BLK, BLK), f32),
            pltpu.VMEM((4, 8, BLK), f32),
            pltpu.VMEM((7, 8, BLK), f32),
            pltpu.VMEM((7, 8, BLK), f32),
            pltpu.VMEM((7, 8, BLK), f32),
            dma((6,)),
            dma((9,)), dma((9,)), dma((8,)), dma((8,)), dma((2, 8)), dma((2, 8)),
            dma((1,)), dma((1,)), dma((9,)), dma((9,)), dma((8,)), dma((8, 2)), dma((8,)), dma((8,)),
            dma((2,)), dma((2,)), dma((2, 2)), dma((2, 2)), dma((24,)), dma((24,)),
        ],
        compiler_params=pltpu.CompilerParams(
            collective_id=0, has_side_effects=True, vmem_limit_bytes=60 << 20
        ),
        name="davidson",
    )(sector_size, wavefunction, left, right)
    return wide[: 2 * BLK].astype(bf), wide[2 * BLK :].astype(bf)


def solution(mesh):
    return jax.shard_map(
        shards,
        mesh=mesh,
        in_specs=(
            P("terms", "sectors"),
            P("terms", "sectors", None, None),
            P("terms", "sectors", None, None),
            P(),
        ),
        out_specs=(P("terms", "sectors"), P("terms", "sectors")),
        check_vma=False,
    )
```

```python
import jax
import jax.numpy as jnp
from jax import lax
from jax.experimental import pallas as pl
from jax.experimental.pallas import tpu as pltpu
from jax.sharding import PartitionSpec as P

MESH = pl.DeviceIdType.MESH
BLK = 128
X, Y, Z = 4, 8, 8
R_RELAY = {0: ((1, 1), (-1, 2)), 1: ((1, 3),), 2: ((-1, 4),), 3: ((1, 5),), 4: ((-1, 6),), 5: ((1, 7),), 6: ((-1, 7),)}
L_RELAY = {0: ((1, 1), (-1, 2), (2, 3), (-2, 4)), 1: ((2, 5),), 2: ((-2, 6),), 3: ((2, 7),), 4: ((-2, 7),)}
OFFS = (0, -1, 1, -2, 2, -3, 3, 4)


def wrap(value, n):
    return lax.rem(value + 2 * n, n)


def device(x, y, z, c):
    return {"terms": 2 * y + c, "sectors": 4 * z + x}


def kernel(
    size_hbm, v_hbm, l_hbm, r_hbm, out,
    sizes, v_own, l_own, rb, ls, vc, im, s1, g, s1h, gh, part, x_in, y_in, z_in,
    local, ry_s, ry_r, rx_s, rx_r, rd_s, rd_r,
    la_s, la_r, lz_s, lz_r, lx_s, lx_r, ld_s, ld_r, v_s, v_r, h_s, h_r, t_s, t_r,
):
    t, s = lax.axis_index("terms"), lax.axis_index("sectors")
    y, c = t // 2, lax.rem(t, 2)
    z, x = s // 4, lax.rem(s, 4)
    other = 1 - c
    xl, xr = x + 1 - 2 * lax.rem(x, 2), 3 - x
    lcore = lax.rem(x, 2)
    own_l = c == lcore
    not_own_l = jnp.logical_not(own_l)
    lslot = jnp.where(own_l, 0, 1)
    hcore = x // 2
    own_v = c == hcore
    diag = y == z
    off_diag = jnp.logical_not(diag)

    barrier = pltpu.get_barrier_semaphore()
    peers = [device(x, y, z, other)]
    for d in (1, 2, 3):
        for e in (0, 1):
            peers.append(device(wrap(x + d, X), y, z, e))
    for d in range(1, 8):
        peers.append(device(x, wrap(y + d, Y), z, c))
        peers.append(device(x, y, wrap(z + d, Z), c))
    across = device(x, z, y, c)

    def hello(to):
        pl.semaphore_signal(barrier, inc=1, device_id=to, device_id_type=MESH)

    pl.when(off_diag)(lambda: hello(across))
    for p in reversed(peers):
        hello(p)

    get_sizes = pltpu.make_async_copy(size_hbm, sizes, local.at[0])
    get_sizes.start()
    own_r = pltpu.make_async_copy(r_hbm, rb.at[0, pl.ds(4 * y + 2 * c, 2)], local.at[1])
    own_r.start()
    get_l = pltpu.make_async_copy(l_hbm, l_own, local.at[2])
    get_l.start()
    get_v = pltpu.make_async_copy(v_hbm, v_own, local.at[3])
    get_v.start()
    get_sizes.wait()
    own_r.wait()
    get_l.wait()
    get_v.wait()
    pl.semaphore_wait(barrier, len(peers) + jnp.where(diag, 0, 1))

    sent = []

    def send(src, dst, ssem, rsem, to, when=None):
        cp = pltpu.make_async_remote_copy(
            src_ref=src, dst_ref=dst, send_sem=ssem, recv_sem=rsem, device_id=to, device_id_type=MESH
        )
        if when is None:
            cp.start()
        else:
            pl.when(when)(lambda: cp.start())
        sent.append((cp, when))

    def got(dst, rsem, when=None):
        cp = pltpu.make_async_remote_copy(
            src_ref=dst, dst_ref=dst, send_sem=rsem, recv_sem=rsem,
            device_id=device(x, y, z, other), device_id_type=MESH,
        )
        if when is None:
            cp.wait_recv()
        else:
            pl.when(when)(lambda: cp.wait_recv())

    yq = [wrap(y + o, Y) for o in OFFS]
    wr = [4 * v + 2 * c for v in yq]
    wo = [4 * v + 2 * other for v in yq]
    sibling = device(x, y, z, other)

    def pass_r(q, step, to_q):
        to = device(x, wrap(y + step, Y), z, c)
        if to_q < 7:
            ref = rb.at[0, pl.ds(wr[q], 2)]
            send(ref, ref, ry_s.at[to_q], ry_r.at[to_q], to)
        else:
            i = 0 if step > 0 else 1
            half = rb.at[0, wr[q] + i]
            send(half, half, ry_s.at[7 + i], ry_r.at[7 + i], to)

    def got_r(q):
        if q < 7:
            got(rb.at[0, pl.ds(wr[q], 2)], ry_r.at[q])
        else:
            for i in (0, 1):
                got(rb.at[0, wr[q] + i], ry_r.at[7 + i])

    def spread_r(q):
        ref = rb.at[0, pl.ds(wr[q], 2)]
        send(ref, rb.at[1, pl.ds(wr[q], 2)], rx_s.at[q], rx_r.at[q], device(xr, y, z, c))
        send(ref, ref, rd_s.at[0, q], rd_r.at[0, q], sibling)

    def beyond(q):
        ref = rb.at[1, pl.ds(wr[q], 2)]
        got(ref, rx_r.at[q])
        send(ref, ref, rd_s.at[1, q], rd_r.at[1, q], sibling)

    def got_far(q):
        for k in (0, 1):
            got(rb.at[k, pl.ds(wo[q], 2)], rd_r.at[k, q])

    zq = [wrap(z + o, Z) for o in OFFS]
    wz = [4 * v + 2 * c for v in zq]
    wzo = [4 * v + 2 * other for v in zq]

    def start_l():
        dst = ls.at[lslot, pl.ds(4 * y + 2 * c, 2)]
        send(l_own, dst, la_s.at[0], la_r.at[0], across, when=off_diag)
        cp = pltpu.make_async_copy(l_own, dst, local.at[2])
        pl.when(diag)(lambda: cp.start())

    def pass_l(q, step, to_q):
        to = device(x, y, wrap(z + step, Z), c)
        if to_q < 7:
            ref = ls.at[lslot, pl.ds(wz[q], 2)]
            send(ref, ref, lz_s.at[to_q], lz_r.at[to_q], to)
        else:
            i = 0 if step > 0 else 1
            half = ls.at[lslot, wz[q] + i]
            send(half, half, lz_s.at[7 + i], lz_r.at[7 + i], to)

    def got_l(q):
        ref = ls.at[lslot, pl.ds(wz[q], 2)]
        if q == 0:
            cp = pltpu.make_async_copy(l_own, ref, local.at[2])
            pl.when(diag)(lambda: cp.wait())
            got(ref, la_r.at[0], when=off_diag)
        elif q < 7:
            got(ref, lz_r.at[q])
        else:
            for i in (0, 1):
                got(ls.at[lslot, wz[q] + i], lz_r.at[7 + i])

    def do_l(q):
        got_l(q)
        for step, to_q in L_RELAY.get(q, ()):
            pass_l(q, step, to_q)
        ref = ls.at[lslot, pl.ds(wz[q], 2)]
        dst = ls.at[0, pl.ds(wz[q], 2)]
        send(ref, dst, lx_s.at[q], lx_r.at[q, c], device(xl, y, z, lcore))
        send(ref, dst, ld_s.at[q], ld_r.at[q], sibling, when=not_own_l)

    def got_l_other(q):
        got(ls.at[0, pl.ds(wzo[q], 2)], ld_r.at[q], when=own_l)
        for e in (0, 1):
            got(ls.at[0, pl.ds(4 * zq[q] + 2 * e, 2)], lx_r.at[q, e], when=not_own_l)

    def do_r(q):
        got_r(q)
        for step, to_q in R_RELAY.get(q, ()):
            pass_r(q, step, to_q)
        spread_r(q)

    start_l()
    for step, to_q in R_RELAY[0]:
        pass_r(0, step, to_q)
    spread_r(0)
    v_chip = jnp.where(own_v, x, xr)
    v_slot = jnp.where(own_v, 0, 1)
    for k in (0, 1):
        keep = jnp.logical_and(own_v, c == k)
        src = v_own.at[pl.ds(BLK * k, BLK)]
        send(
            src, vc.at[v_slot], v_s.at[k], v_r.at[v_slot],
            device(v_chip, y, z, k), when=jnp.logical_not(keep),
        )
        cp = pltpu.make_async_copy(src, vc.at[0], local.at[3])
        pl.when(keep)(lambda: cp.start())
    do_r(1)
    do_r(2)
    beyond(0)
    do_l(0)
    do_r(3)
    beyond(1)
    do_r(4)
    beyond(2)
    do_r(5)
    do_r(6)
    beyond(3)
    beyond(4)
    do_l(1)
    do_l(2)
    do_r(7)
    do_l(3)
    do_l(4)
    beyond(5)
    beyond(6)
    do_l(5)
    do_l(6)
    beyond(7)
    do_l(7)

    got(vc.at[0], v_r.at[0], when=jnp.logical_not(own_v))
    own_block = pltpu.make_async_copy(vc.at[0], vc.at[0], local.at[3])
    pl.when(own_v)(lambda: own_block.wait())
    got(vc.at[1], v_r.at[1])
    rows = lax.broadcasted_iota(jnp.int32, (BLK, BLK), 0)
    cols = lax.broadcasted_iota(jnp.int32, (BLK, BLK), 1)
    row_live = rows < sizes[4 * y + 2 * hcore + c]
    masks = [jnp.logical_and(row_live, cols < sizes[4 * z + n]) for n in (x, xr)]
    v = [jnp.where(masks[k], vc[k].astype(jnp.float32), 0.0) for k in (0, 1)]

    def left(group, both):
        a = ls[0, pl.ds(4 * group, 4)].reshape(4 * BLK, BLK)
        p = jnp.dot(a, both, preferred_element_type=jnp.float32)
        im[pl.ds(4 * group, 4)] = p.astype(jnp.bfloat16).reshape(4, BLK, 2 * BLK)

    def right(group, acc):
        new = []
        for k in (0, 1):
            a = jnp.concatenate(
                [im[4 * group + i, :, pl.ds(BLK * k, BLK)] for i in range(4)], axis=1
            )
            b = jnp.concatenate([rb[k, 4 * group + i] for i in range(4)], axis=1)
            p = lax.dot_general(a, b, (((1,), (1,)), ((), ())), preferred_element_type=jnp.float32)
            new.append(acc[k] + p)
        return tuple(new)

    zero = (jnp.zeros((BLK, BLK), jnp.float32),) * 2
    both = jnp.concatenate([b.astype(jnp.bfloat16) for b in v], axis=1)
    for q in range(5):
        got_l_other(q)
        left(zq[q], both)
    for q in range(8):
        got_far(q)
    total = zero
    for q in range(5):
        total = right(zq[q], total)
    for q in range(5, 8):
        got_l_other(q)
        left(zq[q], both)
        total = right(zq[q], total)

    first = [jnp.where(masks[k], total[k], 0.0) for k in (0, 1)]
    first_b = [f.astype(jnp.bfloat16).astype(jnp.float32) for f in first]

    def fold(a):
        return jnp.sum(a.reshape(BLK // 8, 8, BLK), axis=0)

    def fold_more(a):
        return a[:4] + a[4:]

    num = fold_more(fold(v[0] * first_b[0]) + fold(v[1] * first_b[1]))
    den = fold_more(fold(v[0] * v[0]) + fold(v[1] * v[1]))
    part[0] = jnp.concatenate([num, den], axis=0)

    def swap(n, buf, devs):
        for i, to in enumerate(devs):
            send(part.at[n], buf.at[i], t_s.at[8 * n + i], t_r.at[8 * n + i], to)

    def add(n, buf):
        acc = part[n]
        for i in range(7):
            got(buf.at[i], t_r.at[8 * n + i])
            acc = acc + buf[i]
        part[n + 1] = acc

    swap(0, x_in, [device(wrap(x + d // 2, X), y, z, wrap(c + d, 2)) for d in range(1, 8)])

    num0, den0 = jnp.sum(num), jnp.sum(den)
    theta0 = jnp.where(den0 > 0.0, num0 / jnp.where(den0 > 0.0, den0, 1.0), 0.0)

    def go_home(k, src, dst, n):
        to = device((x, xr)[k], y, z, hcore)
        if k == 0:
            send(src.at[0], dst.at[c], h_s.at[n, 0], h_r.at[n, c], to, when=jnp.logical_not(own_v))
            cp = pltpu.make_async_copy(src.at[0], dst.at[c], local.at[4 + n])
            pl.when(own_v)(lambda: cp.start())
        else:
            send(src.at[1], dst.at[c], h_s.at[n, 1], h_r.at[n, c], to)

    def got_home(dst, n):
        for k in (0, 1):
            keep = jnp.logical_and(own_v, c == k)
            got(dst.at[k], h_r.at[n, k], when=jnp.logical_not(keep))
            cp = pltpu.make_async_copy(dst.at[k], dst.at[k], local.at[4 + n])
            pl.when(keep)(lambda: cp.wait())

    for k in (0, 1):
        s1[k, pl.ds(0, BLK)] = first[k]
        s1[k, pl.ds(BLK, 8)] = jnp.full((8, BLK), theta0, jnp.float32)
        go_home(k, s1, s1h, 0)

    corr = jnp.concatenate([(first_b[k] - theta0 * v[k]).astype(jnp.bfloat16) for k in (0, 1)], axis=1)

    def left_loop(i, carry):
        left(i, corr)
        return carry

    lax.fori_loop(0, 8, left_loop, 0)
    add(0, x_in)
    swap(1, y_in, [device(x, wrap(y + d, Y), z, c) for d in (4, 3, 5, 2, 6, 1, 7)])
    total2 = lax.fori_loop(0, 8, right, zero)
    for k in (0, 1):
        g[k] = jnp.where(masks[k], total2[k], 0.0)
        go_home(k, g, gh, 1)
    add(1, y_in)
    swap(2, z_in, [device(x, y, wrap(z + d, Z), c) for d in (4, 3, 5, 2, 6, 1, 7)])

    got_home(s1h, 0)
    got_home(gh, 1)
    for k in (0, 1):
        out[pl.ds(BLK * k, BLK)] = s1h[k, pl.ds(0, BLK)]
    for cp, when in sent:
        if when is None:
            cp.wait_send()
        else:
            pl.when(when)(lambda cp=cp: cp.wait_send())
    add(2, z_in)
    sums = part[3]
    theta = jnp.sum(sums[:4], keepdims=True) / jnp.sum(sums[4:], keepdims=True)
    home_live = cols < sizes[4 * z + x]
    for k in (0, 1):
        mask = jnp.logical_and(rows < sizes[4 * y + 2 * c + k], home_live)
        shift = theta - s1h[k, pl.ds(BLK, 1)]
        new = gh[k] - shift * s1h[k, pl.ds(0, BLK)]
        out[pl.ds(BLK * (k + 2), BLK)] = jnp.where(mask, new, 0.0)


def shards(wavefunction, left_env, right_env, sector_size):
    left = left_env.reshape(2, BLK, BLK)
    right = right_env.reshape(2, BLK, BLK)
    bf, f32 = jnp.bfloat16, jnp.float32
    hbm = pl.BlockSpec(memory_space=pltpu.MemorySpace.HBM)
    vmem = pl.BlockSpec(memory_space=pltpu.VMEM)
    dma = pltpu.SemaphoreType.DMA
    wide = pl.pallas_call(
        kernel,
        out_shape=jax.ShapeDtypeStruct((4 * BLK, BLK), f32),
        in_specs=[hbm, hbm, hbm, hbm],
        out_specs=vmem,
        scratch_shapes=[
            pltpu.SMEM((32,), jnp.int32),
            pltpu.VMEM((2 * BLK, BLK), bf),
            pltpu.VMEM((2, BLK, BLK), bf),
            pltpu.VMEM((2, 32, BLK, BLK), bf),
            pltpu.VMEM((2, 32, BLK, BLK), bf),
            pltpu.VMEM((2, BLK, BLK), bf),
            pltpu.VMEM((32, BLK, 2 * BLK), bf),
            pltpu.VMEM((2, BLK + 8, BLK), f32),
            pltpu.VMEM((2, BLK, BLK), f32),
            pltpu.VMEM((2, BLK + 8, BLK), f32),
            pltpu.VMEM((2, BLK, BLK), f32),
            pltpu.VMEM((4, 8, BLK), f32),
            pltpu.VMEM((7, 8, BLK), f32),
            pltpu.VMEM((7, 8, BLK), f32),
            pltpu.VMEM((7, 8, BLK), f32),
            dma((6,)),
            dma((9,)), dma((9,)), dma((8,)), dma((8,)), dma((2, 8)), dma((2, 8)),
            dma((1,)), dma((1,)), dma((9,)), dma((9,)), dma((8,)), dma((8, 2)), dma((8,)), dma((8,)),
            dma((2,)), dma((2,)), dma((2, 2)), dma((2, 2)), dma((24,)), dma((24,)),
        ],
        compiler_params=pltpu.CompilerParams(
            collective_id=0, has_side_effects=True, vmem_limit_bytes=60 << 20
        ),
        name="davidson",
    )(sector_size, wavefunction, left, right)
    return wide[: 2 * BLK].astype(bf), wide[2 * BLK :].astype(bf)


def solution(mesh):
    return jax.shard_map(
        shards,
        mesh=mesh,
        in_specs=(
            P("terms", "sectors"),
            P("terms", "sectors", None, None),
            P("terms", "sectors", None, None),
            P(),
        ),
        out_specs=(P("terms", "sectors"), P("terms", "sectors")),
        check_vma=False,
    )
```

```python
import jax
import jax.numpy as jnp
from jax import lax
from jax.experimental import pallas as pl
from jax.experimental.pallas import tpu as pltpu
from jax.sharding import PartitionSpec as P

MESH = pl.DeviceIdType.MESH
BLK = 128
X, Y, Z = 4, 8, 8
R_RELAY = {0: ((1, 1), (-1, 2)), 1: ((1, 3),), 2: ((-1, 4),), 3: ((1, 5),), 4: ((-1, 6),), 5: ((1, 7),), 6: ((-1, 7),)}
L_RELAY = {0: ((1, 1), (-1, 2), (2, 3), (-2, 4)), 1: ((2, 5),), 2: ((-2, 6),), 3: ((2, 7),), 4: ((-2, 7),)}
OFFS = (0, -1, 1, -2, 2, -3, 3, 4)


def wrap(value, n):
    return lax.rem(value + 2 * n, n)


def device(x, y, z, c):
    return {"terms": 2 * y + c, "sectors": 4 * z + x}


def kernel(
    size_hbm, v_hbm, l_hbm, r_hbm, out,
    sizes, v_own, l_own, rb, ls, vc, im, s1, g, s1h, gh, part, x_in, y_in, z_in,
    local, ry_s, ry_r, rx_s, rx_r, rd_s, rd_r,
    la_s, la_r, lz_s, lz_r, lx_s, lx_r, ld_s, ld_r, v_s, v_r, h_s, h_r, t_s, t_r,
):
    t, s = lax.axis_index("terms"), lax.axis_index("sectors")
    y, c = t // 2, lax.rem(t, 2)
    z, x = s // 4, lax.rem(s, 4)
    other = 1 - c
    xl, xr = x + 1 - 2 * lax.rem(x, 2), 3 - x
    lcore = lax.rem(x, 2)
    own_l = c == lcore
    not_own_l = jnp.logical_not(own_l)
    lslot = jnp.where(own_l, 0, 1)
    hcore = x // 2
    own_v = c == hcore
    diag = y == z
    off_diag = jnp.logical_not(diag)

    barrier = pltpu.get_barrier_semaphore()
    peers = [device(x, y, z, other)]
    for d in (1, 2, 3):
        for e in (0, 1):
            peers.append(device(wrap(x + d, X), y, z, e))
    for d in range(1, 8):
        peers.append(device(x, wrap(y + d, Y), z, c))
        peers.append(device(x, y, wrap(z + d, Z), c))
    across = device(x, z, y, c)

    def hello(to):
        pl.semaphore_signal(barrier, inc=1, device_id=to, device_id_type=MESH)

    pl.when(off_diag)(lambda: hello(across))
    for p in reversed(peers):
        hello(p)

    get_sizes = pltpu.make_async_copy(size_hbm, sizes, local.at[0])
    get_sizes.start()
    own_r = pltpu.make_async_copy(r_hbm, rb.at[0, pl.ds(4 * y + 2 * c, 2)], local.at[1])
    own_r.start()
    get_l = pltpu.make_async_copy(l_hbm, l_own, local.at[2])
    get_l.start()
    get_v = pltpu.make_async_copy(v_hbm, v_own, local.at[3])
    get_v.start()
    get_sizes.wait()
    own_r.wait()
    get_l.wait()
    get_v.wait()
    pl.semaphore_wait(barrier, len(peers) + jnp.where(diag, 0, 1))

    sent = []

    def send(src, dst, ssem, rsem, to, when=None):
        cp = pltpu.make_async_remote_copy(
            src_ref=src, dst_ref=dst, send_sem=ssem, recv_sem=rsem, device_id=to, device_id_type=MESH
        )
        if when is None:
            cp.start()
        else:
            pl.when(when)(lambda: cp.start())
        sent.append((cp, when))

    def got(dst, rsem, when=None):
        cp = pltpu.make_async_remote_copy(
            src_ref=dst, dst_ref=dst, send_sem=rsem, recv_sem=rsem,
            device_id=device(x, y, z, other), device_id_type=MESH,
        )
        if when is None:
            cp.wait_recv()
        else:
            pl.when(when)(lambda: cp.wait_recv())

    yq = [wrap(y + o, Y) for o in OFFS]
    wr = [4 * v + 2 * c for v in yq]
    wo = [4 * v + 2 * other for v in yq]
    sibling = device(x, y, z, other)

    def pass_r(q, step, to_q):
        to = device(x, wrap(y + step, Y), z, c)
        if to_q < 7:
            ref = rb.at[0, pl.ds(wr[q], 2)]
            send(ref, ref, ry_s.at[to_q], ry_r.at[to_q], to)
        else:
            i = 0 if step > 0 else 1
            half = rb.at[0, wr[q] + i]
            send(half, half, ry_s.at[7 + i], ry_r.at[7 + i], to)

    def got_r(q):
        if q < 7:
            got(rb.at[0, pl.ds(wr[q], 2)], ry_r.at[q])
        else:
            for i in (0, 1):
                got(rb.at[0, wr[q] + i], ry_r.at[7 + i])

    def spread_r(q):
        ref = rb.at[0, pl.ds(wr[q], 2)]
        send(ref, rb.at[1, pl.ds(wr[q], 2)], rx_s.at[q], rx_r.at[q], device(xr, y, z, c))
        send(ref, ref, rd_s.at[0, q], rd_r.at[0, q], sibling)

    def beyond(q):
        ref = rb.at[1, pl.ds(wr[q], 2)]
        got(ref, rx_r.at[q])
        send(ref, ref, rd_s.at[1, q], rd_r.at[1, q], sibling)

    def got_far(q):
        for k in (0, 1):
            got(rb.at[k, pl.ds(wo[q], 2)], rd_r.at[k, q])

    zq = [wrap(z + o, Z) for o in OFFS]
    wz = [4 * v + 2 * c for v in zq]
    wzo = [4 * v + 2 * other for v in zq]

    def start_l():
        dst = ls.at[lslot, pl.ds(4 * y + 2 * c, 2)]
        send(l_own, dst, la_s.at[0], la_r.at[0], across, when=off_diag)
        cp = pltpu.make_async_copy(l_own, dst, local.at[2])
        pl.when(diag)(lambda: cp.start())

    def pass_l(q, step, to_q):
        to = device(x, y, wrap(z + step, Z), c)
        if to_q < 7:
            ref = ls.at[lslot, pl.ds(wz[q], 2)]
            send(ref, ref, lz_s.at[to_q], lz_r.at[to_q], to)
        else:
            i = 0 if step > 0 else 1
            half = ls.at[lslot, wz[q] + i]
            send(half, half, lz_s.at[7 + i], lz_r.at[7 + i], to)

    def got_l(q):
        ref = ls.at[lslot, pl.ds(wz[q], 2)]
        if q == 0:
            cp = pltpu.make_async_copy(l_own, ref, local.at[2])
            pl.when(diag)(lambda: cp.wait())
            got(ref, la_r.at[0], when=off_diag)
        elif q < 7:
            got(ref, lz_r.at[q])
        else:
            for i in (0, 1):
                got(ls.at[lslot, wz[q] + i], lz_r.at[7 + i])

    def do_l(q):
        got_l(q)
        for step, to_q in L_RELAY.get(q, ()):
            pass_l(q, step, to_q)
        ref = ls.at[lslot, pl.ds(wz[q], 2)]
        dst = ls.at[0, pl.ds(wz[q], 2)]
        send(ref, dst, lx_s.at[q], lx_r.at[q, c], device(xl, y, z, lcore))
        send(ref, dst, ld_s.at[q], ld_r.at[q], sibling, when=not_own_l)

    def got_l_other(q):
        got(ls.at[0, pl.ds(wzo[q], 2)], ld_r.at[q], when=own_l)
        for e in (0, 1):
            got(ls.at[0, pl.ds(4 * zq[q] + 2 * e, 2)], lx_r.at[q, e], when=not_own_l)

    def do_r(q):
        got_r(q)
        for step, to_q in R_RELAY.get(q, ()):
            pass_r(q, step, to_q)
        spread_r(q)

    start_l()
    for step, to_q in R_RELAY[0]:
        pass_r(0, step, to_q)
    spread_r(0)
    v_chip = jnp.where(own_v, x, xr)
    v_slot = jnp.where(own_v, 0, 1)
    for k in (0, 1):
        keep = jnp.logical_and(own_v, c == k)
        src = v_own.at[pl.ds(BLK * k, BLK)]
        send(
            src, vc.at[v_slot], v_s.at[k], v_r.at[v_slot],
            device(v_chip, y, z, k), when=jnp.logical_not(keep),
        )
        cp = pltpu.make_async_copy(src, vc.at[0], local.at[3])
        pl.when(keep)(lambda: cp.start())
    do_r(1)
    do_r(2)
    beyond(0)
    do_l(0)
    do_r(3)
    beyond(1)
    do_r(4)
    beyond(2)
    do_r(5)
    beyond(3)
    do_r(6)
    beyond(4)
    do_l(1)
    do_l(2)
    do_r(7)
    beyond(5)
    do_l(3)
    do_l(4)
    beyond(6)
    do_l(5)
    do_l(6)
    beyond(7)
    do_l(7)

    got(vc.at[0], v_r.at[0], when=jnp.logical_not(own_v))
    own_block = pltpu.make_async_copy(vc.at[0], vc.at[0], local.at[3])
    pl.when(own_v)(lambda: own_block.wait())
    got(vc.at[1], v_r.at[1])
    rows = lax.broadcasted_iota(jnp.int32, (BLK, BLK), 0)
    cols = lax.broadcasted_iota(jnp.int32, (BLK, BLK), 1)
    row_live = rows < sizes[4 * y + 2 * hcore + c]
    masks = [jnp.logical_and(row_live, cols < sizes[4 * z + n]) for n in (x, xr)]
    v = [jnp.where(masks[k], vc[k].astype(jnp.float32), 0.0) for k in (0, 1)]

    def left(group, both):
        a = ls[0, pl.ds(4 * group, 4)].reshape(4 * BLK, BLK)
        p = jnp.dot(a, both, preferred_element_type=jnp.float32)
        im[pl.ds(4 * group, 4)] = p.astype(jnp.bfloat16).reshape(4, BLK, 2 * BLK)

    def right(group, acc):
        new = []
        for k in (0, 1):
            a = jnp.concatenate(
                [im[4 * group + i, :, pl.ds(BLK * k, BLK)] for i in range(4)], axis=1
            )
            b = jnp.concatenate([rb[k, 4 * group + i] for i in range(4)], axis=1)
            p = lax.dot_general(a, b, (((1,), (1,)), ((), ())), preferred_element_type=jnp.float32)
            new.append(acc[k] + p)
        return tuple(new)

    zero = (jnp.zeros((BLK, BLK), jnp.float32),) * 2
    both = jnp.concatenate([b.astype(jnp.bfloat16) for b in v], axis=1)
    for q in range(5):
        got_l_other(q)
        left(zq[q], both)
    for q in range(8):
        got_far(q)
    total = zero
    for q in range(5):
        total = right(zq[q], total)
    for q in range(5, 8):
        got_l_other(q)
        left(zq[q], both)
        total = right(zq[q], total)

    first = [jnp.where(masks[k], total[k], 0.0) for k in (0, 1)]
    first_b = [f.astype(jnp.bfloat16).astype(jnp.float32) for f in first]

    def fold(a):
        return jnp.sum(a.reshape(BLK // 8, 8, BLK), axis=0)

    def fold_more(a):
        return a[:4] + a[4:]

    num = fold_more(fold(v[0] * first_b[0]) + fold(v[1] * first_b[1]))
    den = fold_more(fold(v[0] * v[0]) + fold(v[1] * v[1]))
    part[0] = jnp.concatenate([num, den], axis=0)

    def swap(n, buf, devs):
        for i, to in enumerate(devs):
            send(part.at[n], buf.at[i], t_s.at[8 * n + i], t_r.at[8 * n + i], to)

    def add(n, buf):
        acc = part[n]
        for i in range(7):
            got(buf.at[i], t_r.at[8 * n + i])
            acc = acc + buf[i]
        part[n + 1] = acc

    swap(0, x_in, [device(wrap(x + d // 2, X), y, z, wrap(c + d, 2)) for d in range(1, 8)])

    num0, den0 = jnp.sum(num), jnp.sum(den)
    theta0 = jnp.where(den0 > 0.0, num0 / jnp.where(den0 > 0.0, den0, 1.0), 0.0)

    def go_home(k, src, dst, n):
        to = device((x, xr)[k], y, z, hcore)
        if k == 0:
            send(src.at[0], dst.at[c], h_s.at[n, 0], h_r.at[n, c], to, when=jnp.logical_not(own_v))
            cp = pltpu.make_async_copy(src.at[0], dst.at[c], local.at[4 + n])
            pl.when(own_v)(lambda: cp.start())
        else:
            send(src.at[1], dst.at[c], h_s.at[n, 1], h_r.at[n, c], to)

    def got_home(dst, n):
        for k in (0, 1):
            keep = jnp.logical_and(own_v, c == k)
            got(dst.at[k], h_r.at[n, k], when=jnp.logical_not(keep))
            cp = pltpu.make_async_copy(dst.at[k], dst.at[k], local.at[4 + n])
            pl.when(keep)(lambda: cp.wait())

    for k in (0, 1):
        s1[k, pl.ds(0, BLK)] = first[k]
        s1[k, pl.ds(BLK, 8)] = jnp.full((8, BLK), theta0, jnp.float32)
        go_home(k, s1, s1h, 0)

    corr = jnp.concatenate([(first_b[k] - theta0 * v[k]).astype(jnp.bfloat16) for k in (0, 1)], axis=1)

    def left_loop(i, carry):
        left(i, corr)
        return carry

    lax.fori_loop(0, 8, left_loop, 0)
    add(0, x_in)
    swap(1, y_in, [device(x, wrap(y + d, Y), z, c) for d in (4, 3, 5, 2, 6, 1, 7)])
    total2 = lax.fori_loop(0, 8, right, zero)
    for k in (0, 1):
        g[k] = jnp.where(masks[k], total2[k], 0.0)
        go_home(k, g, gh, 1)
    add(1, y_in)
    swap(2, z_in, [device(x, y, wrap(z + d, Z), c) for d in (4, 3, 5, 2, 6, 1, 7)])

    got_home(s1h, 0)
    got_home(gh, 1)
    for k in (0, 1):
        out[pl.ds(BLK * k, BLK)] = s1h[k, pl.ds(0, BLK)]
    for cp, when in sent:
        if when is None:
            cp.wait_send()
        else:
            pl.when(when)(lambda cp=cp: cp.wait_send())
    add(2, z_in)
    sums = part[3]
    theta = jnp.sum(sums[:4], keepdims=True) / jnp.sum(sums[4:], keepdims=True)
    home_live = cols < sizes[4 * z + x]
    for k in (0, 1):
        mask = jnp.logical_and(rows < sizes[4 * y + 2 * c + k], home_live)
        shift = theta - s1h[k, pl.ds(BLK, 1)]
        new = gh[k] - shift * s1h[k, pl.ds(0, BLK)]
        out[pl.ds(BLK * (k + 2), BLK)] = jnp.where(mask, new, 0.0)


def shards(wavefunction, left_env, right_env, sector_size):
    left = left_env.reshape(2, BLK, BLK)
    right = right_env.reshape(2, BLK, BLK)
    bf, f32 = jnp.bfloat16, jnp.float32
    hbm = pl.BlockSpec(memory_space=pltpu.MemorySpace.HBM)
    vmem = pl.BlockSpec(memory_space=pltpu.VMEM)
    dma = pltpu.SemaphoreType.DMA
    wide = pl.pallas_call(
        kernel,
        out_shape=jax.ShapeDtypeStruct((4 * BLK, BLK), f32),
        in_specs=[hbm, hbm, hbm, hbm],
        out_specs=vmem,
        scratch_shapes=[
            pltpu.SMEM((32,), jnp.int32),
            pltpu.VMEM((2 * BLK, BLK), bf),
            pltpu.VMEM((2, BLK, BLK), bf),
            pltpu.VMEM((2, 32, BLK, BLK), bf),
            pltpu.VMEM((2, 32, BLK, BLK), bf),
            pltpu.VMEM((2, BLK, BLK), bf),
            pltpu.VMEM((32, BLK, 2 * BLK), bf),
            pltpu.VMEM((2, BLK + 8, BLK), f32),
            pltpu.VMEM((2, BLK, BLK), f32),
            pltpu.VMEM((2, BLK + 8, BLK), f32),
            pltpu.VMEM((2, BLK, BLK), f32),
            pltpu.VMEM((4, 8, BLK), f32),
            pltpu.VMEM((7, 8, BLK), f32),
            pltpu.VMEM((7, 8, BLK), f32),
            pltpu.VMEM((7, 8, BLK), f32),
            dma((6,)),
            dma((9,)), dma((9,)), dma((8,)), dma((8,)), dma((2, 8)), dma((2, 8)),
            dma((1,)), dma((1,)), dma((9,)), dma((9,)), dma((8,)), dma((8, 2)), dma((8,)), dma((8,)),
            dma((2,)), dma((2,)), dma((2, 2)), dma((2, 2)), dma((24,)), dma((24,)),
        ],
        compiler_params=pltpu.CompilerParams(
            collective_id=0, has_side_effects=True, vmem_limit_bytes=60 << 20
        ),
        name="davidson",
    )(sector_size, wavefunction, left, right)
    return wide[: 2 * BLK].astype(bf), wide[2 * BLK :].astype(bf)


def solution(mesh):
    return jax.shard_map(
        shards,
        mesh=mesh,
        in_specs=(
            P("terms", "sectors"),
            P("terms", "sectors", None, None),
            P("terms", "sectors", None, None),
            P(),
        ),
        out_specs=(P("terms", "sectors"), P("terms", "sectors")),
        check_vma=False,
    )
```
